32 devices in a mesh: region: 4 (over x, core), dom: 8 (over z, y).
Axes of the slice: x: 2, y: 2, z: 4, core: 2. Of those that a mesh axis runs over, the one named last changes fastest.
Arguments:
- embeds: bfloat16 [65536, 256], P(('region', 'dom')), may hold values from -6 to 6
- neighbours: int32 [65536, 8], P(('region', 'dom')), may hold values from 0 to 3071
- halo_send: int32 [256, 128], P(('region', 'dom')), may hold values from 0 to 2047
- gnn_weight: bfloat16 [512, 256], replicated, may hold values from -0.25 to 0.25
- pair_local: int32 [128, 512], P(('region', 'dom')), may hold values from 0 to 2047
- pair_remote: int32 [128, 512], P(('region', 'dom')), may hold values from 0 to 2047
- pair_count: int32 [32, 4], P(('region', 'dom')), may hold values from 1 to 512, as said below
- targets: float32 [128, 512], P(('region', 'dom')), may hold values from -6 to 6
- pair_w1: bfloat16 [512, 256], replicated, may hold values from -0.25 to 0.25
- pair_w2: bfloat16 [256], replicated, may hold values from -0.375 to 0.375
Outputs:
- embeds_grad: bfloat16 [65536, 256], P(('region', 'dom'))
- gnn_grad: float32 [512, 256], replicated
- pair_w1_grad: float32 [512, 256], replicated
- pair_w2_grad: float32 [256], replicated
- loss: float32 [], replicated
The draws below stay inside these ranges and needn't reach their ends.
Inputs may be any that keep to these rules, and one draw needn't show every extreme that they name: `pair_count`: some partition has 512 live slots for some owner region in every draw.
All inputs are finite; a program needn't handle non-finite values.
Results may differ from the reference program's by a relative error of at most 0.0061.
Values may be sent and summed in bfloat16 or wider, within the bound.
No kernel may reach another device: no remote copies, remote signals or barrier semaphores. Data moves between devices by JAX's collectives and lax.ppermute only.
A program may use at most 128 MiB of HBM per device.

```python
import math
import jax
import jax.numpy as jnp
import numpy as np
from jax import lax

NET_DEV = 2048
F = 256
HID = 256
DEG = 8
HALO = 128
CAP = 512
NETS = 65536
N_REGION = 4
N_DOM = 8


def draw_pair_count(key, part):
    devices = N_REGION * N_DOM
    rank = jnp.arange(devices, dtype=jnp.int32)[:, None]
    upper = CAP // 3 + (CAP - CAP // 3) * rank // (devices - 1) + 1
    lower = jnp.maximum(upper // 2, 1)
    first_key = jax.random.fold_in(key, 11)
    second_key = jax.random.fold_in(key, 12)
    third_key = jax.random.fold_in(key, 13)
    raw_bits = jax.random.randint(first_key, (devices, N_REGION), 0, 1 << 20)
    counts = lower + raw_bits % (upper - lower)
    heavy_device = jax.random.randint(second_key, (), devices // 2, devices)
    heavy_region = jax.random.randint(third_key, (), 0, N_REGION)
    counts = counts.at[heavy_device, heavy_region].set(CAP)
    return counts.astype(jnp.int32)


def with_ends(values, key, least, largest):
    extent = values.shape
    spot = [jax.random.randint(jax.random.fold_in(key, axis), (), 0, extent[axis]) for axis in range(len(extent))]
    values = values.at[tuple(spot)].set(least)
    longest = extent.index(max(extent))
    spot[longest] = (spot[longest] + 1) % extent[longest]
    return values.at[tuple(spot)].set(largest)


def block_levels(stream_key, dims, cuts, smallest, high):
    factor_of = 1.0
    for axis_at, blocks in cuts:
        draws = jax.random.uniform(jax.random.fold_in(jax.random.fold_in(stream_key, 6), axis_at), (blocks,), jnp.float32, smallest / len(cuts), high / len(cuts))
        factor_of = factor_of * jnp.repeat(jnp.exp(draws), dims[axis_at] // blocks).reshape((-1,) + (1,) * (len(dims) - 1 - axis_at))
    return factor_of


def rank_bounds(number_of, slope):
    portions = [(1 << 20) // math.isqrt(grade ** slope) + 1 for grade in range(1, number_of + 1)]
    deviation = 1 + sum(portions) // (1 << 30)
    return np.cumsum(np.array([max(1, weight // deviation) for weight in portions]))


def ranked(rng, dims, count, slope):
    listing = rank_bounds(count, slope)
    pick = jax.random.randint(jax.random.fold_in(rng, 1), dims, 0, int(listing[count - 1]))
    grade = jnp.searchsorted(jnp.asarray(listing, jnp.int32), pick, side="right")
    return jax.random.permutation(jax.random.fold_in(rng, 2), count)[grade].astype(jnp.int32)


def bell_draw(key, extent, spread, reach, pieces=(), held_as=jnp.bfloat16):
    result = spread * jax.random.normal(key, extent, jnp.float32)
    if pieces:
        result = result * block_levels(key, extent, pieces, -0.22, 0.18)
    return jnp.clip(result, -reach, reach).astype(held_as)


def setup_inputs(seed: int = 0) -> dict:
    seeds = jax.random.split(jax.random.key(seed), 11)
    return {
        "embeds": bell_draw(seeds[0], (NETS, F), 1.0, 6.0, ((0, 32),)),
        "neighbours": with_ends(jax.random.randint(seeds[1], (NETS, DEG), 0, NET_DEV + N_DOM * HALO), jax.random.fold_in(seeds[1], 1), 0, (NET_DEV + N_DOM * HALO) - 1).astype(jnp.int32),
        "halo_send": with_ends(jax.random.randint(seeds[2], (N_REGION * N_DOM * N_DOM, HALO), 0, NET_DEV), jax.random.fold_in(seeds[2], 1), 0, NET_DEV - 1).astype(jnp.int32),
        "gnn_weight": bell_draw(seeds[3], (2 * F, F), (2 * F) ** -0.5, 0.25),
        "pair_local": with_ends(jax.random.randint(seeds[4], (N_REGION * N_DOM * N_REGION, CAP), 0, NET_DEV), jax.random.fold_in(seeds[4], 1), 0, NET_DEV - 1).astype(jnp.int32),
        "pair_remote": with_ends(ranked(seeds[5], (N_REGION * N_DOM * N_REGION, CAP), NET_DEV, 2), jax.random.fold_in(seeds[5], 3), 0, NET_DEV - 1).astype(jnp.int32),
        "pair_count": draw_pair_count(jax.random.fold_in(seeds[10], 71), 0),
        "targets": bell_draw(seeds[7], (N_REGION * N_DOM * N_REGION, CAP), 1.0, 6.0, ((0, 32),), jnp.float32),
        "pair_w1": bell_draw(seeds[8], (2 * F, HID), (2 * F) ** -0.5, 0.25),
        "pair_w2": bell_draw(seeds[9], (HID,), HID ** -0.5, 0.375),
    }


gelu_coef = 0.7978845608

def gelu_tanh(value):
    inner = jnp.tanh(gelu_coef * (value + 0.044715 * value * value * value))
    return 0.5 * value * (1.0 + inner)

def gelu_slope(value):
    inner = jnp.tanh(gelu_coef * (value + 0.044715 * value * value * value))
    return 0.5 * (1.0 + inner) + 0.5 * value * (1.0 - inner * inner) * gelu_coef * (1.0 + 3.0 * 0.044715 * value * value)

def reference(embeds, neighbours, halo_send, gnn_weight, pair_local, pair_remote, pair_count, targets, pair_w1, pair_w2):
    regions = N_REGION
    doms = N_DOM
    devices = regions * doms
    own_blocks = embeds.reshape(devices, NET_DEV, F)
    neigh_blocks = neighbours.reshape(devices, NET_DEV, DEG)
    send_lists = halo_send.reshape(regions, doms, doms, HALO)
    local_blocks = pair_local.reshape(devices, regions, CAP)
    remote_blocks = pair_remote.reshape(devices, regions, CAP)
    target_blocks = targets.reshape(devices, regions * CAP)
    device_ids = jnp.arange(devices, dtype=jnp.int32)

    def lists_for(device):
        region_at = device // doms
        dom_at = device % doms
        lists = send_lists[region_at][:, dom_at, :]
        senders = region_at * doms + jnp.arange(doms, dtype=jnp.int32)
        return (senders, lists)

    def layer_inputs(device):
        senders, lists = lists_for(device)
        received = own_blocks[senders[:, None], lists]
        table = jnp.concatenate([own_blocks[device], received.reshape(-1, F)], 0)
        agg_sum = jnp.zeros((NET_DEV, F), jnp.float32)
        for column in range(DEG):
            agg_sum = agg_sum + table[neigh_blocks[device][:, column]].astype(jnp.float32)
        aggregate = (agg_sum / DEG).astype(jnp.bfloat16)
        joined = jnp.concatenate([own_blocks[device], aggregate], 1)
        pre = jnp.dot(joined, gnn_weight, preferred_element_type=jnp.float32)
        return (joined, pre)

    def forward(device):
        joined, pre = layer_inputs(device)
        return (own_blocks[device].astype(jnp.float32) + gelu_tanh(pre)).astype(jnp.bfloat16)
    net_blocks = lax.map(forward, device_ids)

    def pair_step(carry, device):
        dnets_all, grad_w1, grad_w2, sq_total = carry
        dom_at = device % doms
        owners = jnp.arange(regions, dtype=jnp.int32) * doms + dom_at
        partner = net_blocks[owners[:, None], remote_blocks[device]]
        victim = net_blocks[device][local_blocks[device]]
        pairs_in = jnp.concatenate([victim, partner], 2).reshape(regions * CAP, 2 * F)
        linear = jnp.dot(pairs_in, pair_w1, preferred_element_type=jnp.float32)
        activated = gelu_tanh(linear).astype(jnp.bfloat16)
        scores = jnp.dot(activated, pair_w2, preferred_element_type=jnp.float32)
        counts = pair_count[device]
        slot_ids = jnp.arange(CAP, dtype=jnp.int32)
        valid_mask = (slot_ids[None, :] < counts[:, None]).astype(jnp.float32).reshape(-1)
        errors = (scores - target_blocks[device]) * valid_mask
        residual = 2.0 * errors
        lin_grad = (residual[:, None] * pair_w2.astype(jnp.float32)[None, :] * gelu_slope(linear)).astype(jnp.bfloat16)
        grad_w1 = grad_w1 + jnp.dot(pairs_in.T, lin_grad, preferred_element_type=jnp.float32)
        grad_w2 = grad_w2 + lax.optimization_barrier(jnp.sum(residual[:, None] * activated.astype(jnp.float32), 0))
        pair_grad = jnp.dot(lin_grad, pair_w1.T, preferred_element_type=jnp.float32)
        victim_grad = pair_grad[:, :F]
        partner_grad = lax.optimization_barrier(pair_grad[:, F:].astype(jnp.bfloat16))
        dnets_all = dnets_all.at[device, local_blocks[device].reshape(-1)].add(victim_grad)
        dnets_all = dnets_all.at[owners[:, None], remote_blocks[device]].add(partner_grad.astype(jnp.float32).reshape(regions, CAP, F))
        return ((dnets_all, grad_w1, grad_w2, sq_total + jnp.sum(errors * errors)), None)
    start = (jnp.zeros((devices, NET_DEV, F), jnp.float32), jnp.zeros((2 * F, HID), jnp.float32), jnp.zeros((HID,), jnp.float32), jnp.zeros((), jnp.float32))
    (dnets_all, grad_w1, grad_w2, sq_total), _ = lax.scan(pair_step, start, device_ids)

    def layer_step(carry, device):
        dembeds_all, grad_gnn = carry
        joined, pre = layer_inputs(device)
        pre_grad = (dnets_all[device] * gelu_slope(pre)).astype(jnp.bfloat16)
        grad_gnn = grad_gnn + jnp.dot(joined.T, pre_grad, preferred_element_type=jnp.float32)
        cat_grad = jnp.dot(pre_grad, gnn_weight.T, preferred_element_type=jnp.float32)
        agg_grad = lax.optimization_barrier((cat_grad[:, F:] / DEG).astype(jnp.bfloat16)).astype(jnp.float32)
        table_grad = jnp.zeros((NET_DEV + doms * HALO, F), jnp.float32)
        for column in range(DEG):
            table_grad = table_grad.at[neigh_blocks[device][:, column]].add(agg_grad)
        senders, lists = lists_for(device)
        dembeds_all = dembeds_all.at[device].add(dnets_all[device] + cat_grad[:, :F] + table_grad[:NET_DEV])
        returned = lax.optimization_barrier(table_grad[NET_DEV:].astype(jnp.bfloat16))
        dembeds_all = dembeds_all.at[senders[:, None], lists].add(returned.astype(jnp.float32).reshape(doms, HALO, F))
        return ((dembeds_all, grad_gnn), None)
    (dembeds_all, grad_gnn), _ = lax.scan(layer_step, (jnp.zeros((devices, NET_DEV, F), jnp.float32), jnp.zeros((2 * F, F), jnp.float32)), device_ids)
    total_count = jnp.sum(pair_count).astype(jnp.float32)
    root_count = jnp.sqrt(total_count)
    embeds_grad = (dembeds_all * (8.0 * NETS / total_count)).astype(jnp.bfloat16).reshape(NETS, F)
    return (embeds_grad, 8.0 * grad_gnn / root_count, 8.0 * grad_w1 / root_count, 8.0 * grad_w2 / root_count, sq_total / total_count)
```

```python
import functools

import jax
import jax.numpy as jnp
from jax import lax
from jax.experimental import pallas as pl
from jax.experimental.pallas import tpu as pltpu
from jax.sharding import PartitionSpec as P

bf16 = jnp.bfloat16
f32 = jnp.float32
i32 = jnp.int32
i16 = jnp.int16
gelu_coef = 0.7978845608
BOTH = ("region", "dom")
BLOCK = 256
TT = (((0,), (0,)), ((), ()))
NT = (((1,), (1,)), ((), ()))


def mm(a, b):
    return jnp.dot(a, b, preferred_element_type=f32)


def mm_dims(a, b, dims):
    return lax.dot_general(a, b, dims, preferred_element_type=f32)


def gelu_inner(value):
    return jnp.tanh(gelu_coef * (value + 0.044715 * value * value * value))


def slope_of(value, inner):
    return 0.5 * (1.0 + inner) + 0.5 * value * (1.0 - inner * inner) * gelu_coef * (
        1.0 + 3.0 * 0.044715 * value * value
    )


def column_of(row):
    return jnp.broadcast_to(row, (128, row.shape[1])).T


def onehot_rows(row, width):
    column = column_of(row).astype(i16)
    lane = lax.broadcasted_iota(i32, column.shape, 1).astype(i16)
    one = jnp.ones(column.shape, bf16)
    zero = jnp.zeros(column.shape, bf16)
    return jnp.concatenate(
        [jnp.where(column == lane + jnp.int16(128 * j), one, zero) for j in range(width // 128)], 1
    )


def onehot_cols(row, first, height):
    shape = (height, row.shape[1])
    wide = jnp.broadcast_to(row - first, shape).astype(i16)
    sub = lax.broadcasted_iota(i32, shape, 0).astype(i16)
    return jnp.where(wide == sub, jnp.ones(shape, bf16), jnp.zeros(shape, bf16))


def halo_gather_kernel(send_ref, embeds_ref, out_ref):
    peers, halo = send_ref.shape
    nets = embeds_ref.shape[0]
    for p in range(peers):
        hot = onehot_rows(send_ref[p : p + 1, :], nets)
        out_ref[p * halo : (p + 1) * halo, :] = mm(hot, embeds_ref[...]).astype(bf16)


def adjacency_kernel(
    neigh_ref, embeds_ref, block_ref, gnn_ref, own_ref, halo_ref, sum_ref, pre_ref
):
    degree = neigh_ref.shape[0]
    rows, nets = own_ref.shape
    feat = embeds_ref.shape[1]
    listed = [neigh_ref[c : c + 1, :] for c in range(degree)]
    columns, counts = [], []
    for c in range(degree):
        count = jnp.ones_like(listed[c])
        seen = None
        for e in range(degree):
            if e != c:
                same = listed[e] == listed[c]
                if e > c:
                    count = count + same.astype(i32)
                else:
                    seen = same if seen is None else (seen | same)
        index = listed[c] if seen is None else jnp.where(seen, -1, listed[c])
        columns.append(column_of(index).astype(i16))
        counts.append(column_of(count).astype(f32).astype(bf16))
    lane = lax.broadcasted_iota(i32, (rows, 128), 1).astype(i16)
    zero = jnp.zeros((rows, 128), bf16)

    def tile(at):
        acc = zero
        here = lane + jnp.int16(at)
        for c in range(degree):
            acc = jnp.where(columns[c] == here, counts[c], acc)
        return acc

    for at in range(0, nets, 128):
        own_ref[:, at : at + 128] = tile(at)
    for at in range(0, halo_ref.shape[1], 128):
        halo_ref[:, at : at + 128] = tile(nets + at)
    sum_ref[...] = mm(own_ref[...], embeds_ref[...])
    pre_ref[...] = mm(block_ref[...], gnn_ref[:feat, :])


def asked_kernel(asked_ref, hot_ref):
    regions, slots = asked_ref.shape
    for q in range(regions):
        hot_ref[q] = onehot_rows(asked_ref[q : q + 1, :], hot_ref.shape[2])


def layer_kernel(
    rid_ref,
    halo_ref,
    received_ref,
    sum_ref,
    pre_own_ref,
    embeds_ref,
    gnn_ref,
    hot_ref,
    pre_ref,
    agg_ref,
    nets_ref,
    *send_refs,
    degree,
):
    nets, feat = embeds_ref.shape
    regions = hot_ref.shape[0]
    for at in range(0, nets, BLOCK):
        rows = slice(at, at + BLOCK)
        total = sum_ref[rows, :] + mm(halo_ref[rows, :], received_ref[...])
        agg = (total / degree).astype(bf16)
        agg_ref[rows, :] = agg
        pre = pre_own_ref[rows, :] + mm(agg, gnn_ref[feat:, :])
        pre_ref[rows, :] = pre
        gelu = 0.5 * pre * (1.0 + gelu_inner(pre))
        nets_ref[rows, :] = (embeds_ref[rows, :].astype(f32) + gelu).astype(bf16)
    me = rid_ref[0]
    for k in [*range(1, regions), 0]:
        send_refs[k][...] = mm(hot_ref[me ^ k], nets_ref[...]).astype(bf16)


def victim_kernel(rid_ref, local_ref, nets_ref, w1_ref, pre_ref, victim_ref, linear_ref, slope_ref):
    regions, slots = local_ref.shape
    nets, feat = nets_ref.shape
    me = rid_ref[0]
    for k in range(regions):
        hot = onehot_rows(local_ref[pl.ds(me ^ k, 1), :], nets)
        victim = mm(hot, nets_ref[...]).astype(bf16)
        victim_ref[k] = victim
        linear_ref[k] = mm(victim, w1_ref[:feat, :])
    for at in range(0, nets, BLOCK):
        pre = pre_ref[at : at + BLOCK, :]
        slope_ref[at : at + BLOCK, :] = slope_of(pre, gelu_inner(pre))


def pair_kernel(rid_ref, count_ref, target_ref, linear_ref, w1_ref, w2_ref, *refs, ks):
    some = len(ks)
    partner_refs, (lin_grad_ref, w2_sum_ref, sq_ref), back_refs = (
        refs[:some],
        refs[some : some + 3],
        refs[some + 3 :],
    )
    me = rid_ref[0]
    slots, hid = linear_ref.shape[1:]
    feat = partner_refs[0].shape[1]
    w2_row = w2_ref[...].astype(f32)
    w2_column = column_of(w2_row).astype(bf16)
    w2_sum = jnp.zeros((1, hid), f32)
    sq_sum = jnp.zeros((1, 128), f32)
    slot = lax.broadcasted_iota(i32, (slots, 128), 0)
    for at, k in enumerate(ks):
        linear = linear_ref[k] + mm(partner_refs[at][...], w1_ref[feat:, :])
        inner = gelu_inner(linear)
        activated = (0.5 * linear * (1.0 + inner)).astype(bf16)
        scores = mm(activated, w2_column)
        live = slot < count_ref[0, me ^ k]
        errors = jnp.where(live, scores - column_of(target_ref[pl.ds(me ^ k, 1), :]), 0.0)
        sq_sum = sq_sum + jnp.sum(errors * errors, 0, keepdims=True)
        residual = 2.0 * errors
        residual = jnp.concatenate([residual] * (hid // 128), 1)
        w2_sum = w2_sum + jnp.sum(residual * activated.astype(f32), 0, keepdims=True)
        lin_grad = (residual * w2_row * slope_of(linear, inner)).astype(bf16)
        lin_grad_ref[at] = lin_grad
        back_refs[at][...] = mm_dims(lin_grad, w1_ref[feat:, :], NT).astype(bf16)
    w2_sum_ref[...] = jnp.broadcast_to(w2_sum, w2_sum_ref.shape)
    sq_ref[...] = jnp.broadcast_to(sq_sum, sq_ref.shape)


def local_grad_kernel(
    rid_ref, local_ref, asked_ref, w1_ref, victim_ref, *refs, regions, groups, near
):
    partner_refs, refs = refs[:regions], refs[regions:]
    lin_refs, refs = refs[: len(groups)], refs[len(groups) :]
    near_refs, refs = refs[:near], refs[near:]
    grad_ref, hot_ref, w1_grad_ref, vg_ref = refs
    me = rid_ref[0]
    slots, feat = victim_ref.shape[1:]
    nets = grad_ref.shape[0]
    top = jnp.zeros((feat, w1_ref.shape[1]), f32)
    low = jnp.zeros((feat, w1_ref.shape[1]), f32)
    for ref, ks in zip(lin_refs, groups, strict=True):
        for at, k in enumerate(ks):
            lin_grad = ref[at]
            vg_ref[k * slots : (k + 1) * slots, :] = mm_dims(lin_grad, w1_ref[:feat, :], NT).astype(
                bf16
            )
            top = top + mm_dims(victim_ref[k], lin_grad, TT)
            low = low + mm_dims(partner_refs[k][...], lin_grad, TT)
    w1_grad_ref[:feat, :] = top.astype(bf16)
    w1_grad_ref[feat:, :] = low.astype(bf16)
    local = [local_ref[pl.ds(me ^ k, 1), :] for k in range(regions)]
    asked = [asked_ref[pl.ds(me ^ k, 1), :] for k in range(regions)]
    for at in range(0, nets, BLOCK):
        hot = jnp.concatenate([onehot_cols(row, at, BLOCK) for row in local], 1)
        total = mm(hot, vg_ref[...])
        for k in range(near):
            total = total + mm(onehot_cols(asked[k], at, BLOCK), near_refs[k][...])
        grad_ref[at : at + BLOCK, :] = total
        for k in range(near, regions):
            hot_ref[at : at + BLOCK, (k - near) * slots : (k - near + 1) * slots] = onehot_cols(
                asked[k], at, BLOCK
            )


def layer_grad_kernel(
    grad_ref, hot_ref, slope_ref, gnn_ref, halo_ref, *refs, far, degree
):
    far_refs, (total_ref, pre_grad_ref, agg_grad_ref, back_ref) = refs[:far], refs[far:]
    nets, feat = grad_ref.shape
    slots = far_refs[0].shape[0]
    for at in range(0, nets, BLOCK):
        rows = slice(at, at + BLOCK)
        total = grad_ref[rows, :]
        for k in range(far):
            total = total + mm(hot_ref[rows, k * slots : (k + 1) * slots], far_refs[k][...])
        total_ref[rows, :] = total
        pre_grad = (total * slope_ref[rows, :]).astype(bf16)
        pre_grad_ref[rows, :] = pre_grad
        agg_grad_ref[:, rows] = (mm_dims(gnn_ref[feat:, :], pre_grad, NT) / degree).astype(bf16)
    for at in range(0, halo_ref.shape[1], BLOCK):
        back = mm(agg_grad_ref[...], halo_ref[:, at : at + BLOCK])
        back_ref[at : at + BLOCK, :] = back.T.astype(bf16)


def gnn_grad_kernel(embeds_ref, agg_ref, pre_grad_ref, out_ref):
    feat = embeds_ref.shape[1]
    out_ref[:feat, :] = mm_dims(embeds_ref[...], pre_grad_ref[...], TT).astype(bf16)
    out_ref[feat:, :] = mm_dims(agg_ref[...], pre_grad_ref[...], TT).astype(bf16)


def own_grad_kernel(total_ref, pre_grad_ref, gnn_ref, agg_grad_ref, own_ref, out_ref):
    feat = agg_grad_ref.shape[0]
    out_ref[...] = (
        total_ref[...]
        + mm_dims(pre_grad_ref[...], gnn_ref[:feat, :], NT)
        + mm(agg_grad_ref[...], own_ref[...]).T
    )


def final_kernel(scale_ref, send_ref, own_ref, returned_ref, out_ref):
    nets = out_ref.shape[0]
    peers = send_ref.shape[0]
    scale = scale_ref[0]
    for at in range(0, nets, BLOCK):
        hot = jnp.concatenate(
            [onehot_cols(send_ref[p : p + 1, :], at, BLOCK) for p in range(peers)], 1
        )
        total = own_ref[at : at + BLOCK, :] + mm(hot, returned_ref[...])
        out_ref[at : at + BLOCK, :] = (total * scale).astype(bf16)


VM = pl.BlockSpec(memory_space=pltpu.VMEM)
SM = pl.BlockSpec(memory_space=pltpu.SMEM)


def params(mib):
    return pltpu.CompilerParams(vmem_limit_bytes=mib << 20)


def cost(flops, moved):
    return pl.CostEstimate(flops=flops, bytes_accessed=moved, transcendentals=0)


def shape(dims, dtype):
    return jax.ShapeDtypeStruct(dims, dtype)


def exchange(value, axis):
    return lax.all_to_all(value, axis, split_axis=0, concat_axis=0, tiled=True)


def two_parts(value):
    high = value.astype(bf16)
    return high, (value - high.astype(f32)).astype(bf16)


def local(
    embeds,
    neighbours,
    halo_send,
    gnn_weight,
    pair_local,
    pair_remote,
    pair_count,
    targets,
    pair_w1,
    pair_w2,
):
    nets, feat = embeds.shape
    hid = pair_w1.shape[1]
    degree = neighbours.shape[1]
    regions, slots = pair_local.shape
    peers, halo = halo_send.shape
    halo_rows = peers * halo
    devices = lax.axis_size("region") * lax.axis_size("dom")
    rid = lax.axis_index("region").astype(i32).reshape(1)
    near = 2

    def permute(value, k):
        return lax.ppermute(value, "region", [(i, i ^ k) for i in range(regions)])

    outgoing = pl.pallas_call(
        halo_gather_kernel,
        out_shape=shape((halo_rows, feat), bf16),
        in_specs=[VM, VM],
        out_specs=VM,
        compiler_params=params(24),
        cost_estimate=cost(2 * halo_rows * nets * feat, 2 << 20),
        name="halo_gather",
    )(halo_send, embeds)
    received = exchange(outgoing.reshape(peers, halo, feat), "dom").reshape(halo_rows, feat)
    asked = exchange(pair_remote.reshape(regions, 1, slots), "region").reshape(regions, slots)

    own, from_halo, agg_sum, pre_own = pl.pallas_call(
        adjacency_kernel,
        grid=(nets // BLOCK,),
        in_specs=[
            pl.BlockSpec((degree, BLOCK), lambda i: (0, i)),
            pl.BlockSpec((nets, feat), lambda i: (0, 0)),
            pl.BlockSpec((BLOCK, feat), lambda i: (i, 0)),
            pl.BlockSpec((2 * feat, feat), lambda i: (0, 0)),
        ],
        out_specs=[
            pl.BlockSpec((BLOCK, nets), lambda i: (i, 0)),
            pl.BlockSpec((BLOCK, halo_rows), lambda i: (i, 0)),
            pl.BlockSpec((BLOCK, feat), lambda i: (i, 0)),
            pl.BlockSpec((BLOCK, feat), lambda i: (i, 0)),
        ],
        out_shape=[
            shape((nets, nets), bf16),
            shape((nets, halo_rows), bf16),
            shape((nets, feat), f32),
            shape((nets, feat), f32),
        ],
        compiler_params=params(24),
        cost_estimate=cost(20 * nets * (nets + halo_rows) * feat // 2, 20 << 20),
        name="adjacency",
    )(neighbours.T, embeds, embeds, gnn_weight)

    asked_hot = pl.pallas_call(
        asked_kernel,
        out_shape=shape((regions, slots, nets), bf16),
        in_specs=[VM],
        out_specs=VM,
        compiler_params=params(40),
        cost_estimate=cost(2 * nets * nets * feat, 8 << 20),
        name="asked_onehot",
    )(asked)

    pre, aggregate, net_values, *sends = pl.pallas_call(
        functools.partial(layer_kernel, degree=degree),
        out_shape=[
            shape((nets, feat), f32),
            shape((nets, feat), bf16),
            shape((nets, feat), bf16),
        ]
        + [shape((slots, feat), bf16)] * regions,
        in_specs=[SM] + [VM] * 7,
        out_specs=[VM] * (3 + regions),
        compiler_params=params(40),
        cost_estimate=cost(2 * nets * nets * feat * 2, 20 << 20),
        name="layer",
    )(rid, from_halo, received, agg_sum, pre_own, embeds, gnn_weight, asked_hot)

    partners = [sends[0]] + [permute(sends[k], k) for k in range(1, regions)]

    victim, linear_own, slope = pl.pallas_call(
        victim_kernel,
        out_shape=[
            shape((regions, slots, feat), bf16),
            shape((regions, slots, hid), f32),
            shape((nets, feat), f32),
        ],
        in_specs=[SM] + [VM] * 4,
        out_specs=[VM] * 3,
        compiler_params=params(40),
        cost_estimate=cost(2 * nets * nets * feat * 2, 8 << 20),
        name="victims",
    )(rid, pair_local, net_values, pair_w1, pre)

    groups = [tuple(range(near))] + [(k,) for k in range(near, regions)]
    w2_row = pair_w2.reshape(1, hid)
    lin_grads, backs, w2_sums, sq_sums = [], [], [], []
    for ks in groups:
        lin_grad, w2_sum, sq_sum, *back = pl.pallas_call(
            functools.partial(pair_kernel, ks=ks),
            out_shape=[
                shape((len(ks), slots, hid), bf16),
                shape((8, hid), f32),
                shape((8, 128), f32),
            ]
            + [shape((slots, feat), bf16)] * len(ks),
            in_specs=[SM, SM] + [VM] * (4 + len(ks)),
            out_specs=[VM] * (3 + len(ks)),
            compiler_params=params(24),
            cost_estimate=cost(len(ks) * 2 * slots * hid * feat * 16, 2 << 20),
            name="pairs",
        )(rid, pair_count, targets, linear_own, pair_w1, w2_row, *[partners[k] for k in ks])
        lin_grads.append(lin_grad)
        backs += back
        w2_sums.append(w2_sum[0])
        sq_sums.append(sq_sum[0, 0])
    returned = [backs[0]] + [permute(backs[k], k) for k in range(1, regions)]

    far = regions - near
    local_grad, far_hot, w1_part = pl.pallas_call(
        functools.partial(local_grad_kernel, regions=regions, groups=groups, near=near),
        out_shape=[
            shape((nets, feat), f32),
            shape((nets, far * slots), bf16),
            shape((2 * feat, hid), bf16),
        ],
        in_specs=[SM] + [VM] * (4 + regions + len(groups) + near),
        out_specs=[VM] * 3,
        scratch_shapes=[pltpu.VMEM((regions * slots, feat), bf16)],
        compiler_params=params(40),
        cost_estimate=cost(2 * nets * nets * feat * 3, 12 << 20),
        name="local_grads",
    )(rid, pair_local, asked, pair_w1, victim, *partners, *lin_grads, *returned[:near])

    share = 2 * feat * hid // devices
    scalars = jnp.zeros((2, 128), f32)
    scalars = scalars.at[0, 0].set(sum(sq_sums)).at[1, 0].set(jnp.sum(pair_count).astype(f32))
    short = jnp.concatenate([sum(w2_sums).reshape(-1, 128), scalars], 0)
    short = jnp.concatenate(two_parts(short), 0)
    short_rows = short.shape[0]
    w1_parts = jnp.concatenate(
        [
            w1_part.reshape(devices, share // 128, 128),
            jnp.broadcast_to(short[None], (devices, short_rows, 128)),
        ],
        1,
    )
    w1_got = jnp.sum(exchange(w1_parts, BOTH).astype(f32), 0)
    short_sum = w1_got[share // 128 :]
    short_sum = short_sum[: short_rows // 2] + short_sum[short_rows // 2 :]
    w2_total = short_sum[: hid // 128].reshape(hid)
    sq_total = short_sum[hid // 128, 0]
    total_count = short_sum[hid // 128 + 1, 0]
    root_count = jnp.sqrt(total_count)

    def spread(value):
        value = (8.0 * value / root_count).astype(bf16)
        wide = jnp.broadcast_to(value[None], (devices,) + value.shape)
        return exchange(wide, BOTH).reshape(2 * feat, hid).astype(f32)

    w1_grad = spread(w1_got[: share // 128])

    total_grad, pre_grad, agg_grad, halo_back = pl.pallas_call(
        functools.partial(layer_grad_kernel, far=far, degree=degree),
        out_shape=[
            shape((nets, feat), f32),
            shape((nets, feat), bf16),
            shape((feat, nets), bf16),
            shape((halo_rows, feat), bf16),
        ],
        in_specs=[VM] * (5 + far),
        out_specs=[VM] * 4,
        compiler_params=params(40),
        cost_estimate=cost(2 * nets * nets * feat * 2, 16 << 20),
        name="layer_grad",
    )(local_grad, far_hot, slope, gnn_weight, from_halo, *returned[near:])
    returned_halo = exchange(halo_back.reshape(peers, halo, feat), "dom").reshape(halo_rows, feat)

    gnn_part = pl.pallas_call(
        gnn_grad_kernel,
        out_shape=shape((2 * feat, feat), bf16),
        in_specs=[VM] * 3,
        out_specs=VM,
        compiler_params=params(24),
        cost_estimate=cost(2 * nets * 2 * feat * feat * 3, 4 << 20),
        name="gnn_grads",
    )(embeds, aggregate, pre_grad)
    gnn_got = jnp.sum(exchange(gnn_part.reshape(devices, share // 128, 128), BOTH).astype(f32), 0)
    gnn_grad = spread(gnn_got)

    own_grad = pl.pallas_call(
        own_grad_kernel,
        grid=(nets // BLOCK,),
        in_specs=[
            pl.BlockSpec((BLOCK, feat), lambda i: (i, 0)),
            pl.BlockSpec((BLOCK, feat), lambda i: (i, 0)),
            pl.BlockSpec((2 * feat, feat), lambda i: (0, 0)),
            pl.BlockSpec((feat, nets), lambda i: (0, 0)),
            pl.BlockSpec((nets, BLOCK), lambda i: (0, i)),
        ],
        out_specs=pl.BlockSpec((BLOCK, feat), lambda i: (i, 0)),
        out_shape=shape((nets, feat), f32),
        compiler_params=params(24),
        cost_estimate=cost(2 * nets * nets * feat * 2, 12 << 20),
        name="own_grads",
    )(total_grad, pre_grad, gnn_weight, agg_grad, own)

    scale = (8.0 * nets * devices / total_count).reshape(1)
    embeds_grad = pl.pallas_call(
        final_kernel,
        out_shape=shape((nets, feat), bf16),
        in_specs=[SM] + [VM] * 3,
        out_specs=VM,
        compiler_params=params(24),
        cost_estimate=cost(2 * nets * halo_rows * feat * 2, 6 << 20),
        name="embeds_grads",
    )(scale, halo_send, own_grad, returned_halo)
    return (
        embeds_grad,
        gnn_grad,
        w1_grad,
        8.0 * w2_total / root_count,
        sq_total / total_count,
    )


def solution(mesh):
    split = P(BOTH, None)
    in_specs = (split, split, split, P(), split, split, split, split, P(), P())
    out_specs = (split, P(), P(), P(), P())
    return jax.shard_map(local, mesh=mesh, in_specs=in_specs, out_specs=out_specs, check_vma=False)
```

```python
import functools

import jax
import jax.numpy as jnp
from jax import lax
from jax.experimental import pallas as pl
from jax.experimental.pallas import tpu as pltpu
from jax.sharding import PartitionSpec as P

bf16 = jnp.bfloat16
f32 = jnp.float32
i32 = jnp.int32
i16 = jnp.int16
gelu_coef = 0.7978845608
BOTH = ("region", "dom")
BLOCK = 256
STEP = 512
TT = (((0,), (0,)), ((), ()))
NT = (((1,), (1,)), ((), ()))


def mm(a, b):
    return jnp.dot(a, b, preferred_element_type=f32)


def mm_dims(a, b, dims):
    return lax.dot_general(a, b, dims, preferred_element_type=f32)


def gelu_inner(value, square):
    return jnp.tanh(value * (gelu_coef + (gelu_coef * 0.044715) * square))


def gelu_of(value):
    half = 0.5 * value
    return half + half * gelu_inner(value, value * value)


def slope_of(value, square, inner):
    rise = value * (0.5 * gelu_coef + (1.5 * 0.044715 * gelu_coef) * square)
    return 0.5 + 0.5 * inner + (1.0 - inner * inner) * rise


def column_of(row):
    return jnp.broadcast_to(row, (128, row.shape[1])).T


def onehot_rows(row, width):
    column = column_of(row).astype(i16)
    lane = lax.broadcasted_iota(i32, column.shape, 1).astype(i16)
    one = jnp.ones(column.shape, bf16)
    zero = jnp.zeros(column.shape, bf16)
    return jnp.concatenate(
        [jnp.where(column == lane + jnp.int16(128 * j), one, zero) for j in range(width // 128)], 1
    )


def onehot_cols(row, first, height):
    shape = (height, row.shape[1])
    wide = jnp.broadcast_to(row - first, shape).astype(i16)
    sub = lax.broadcasted_iota(i32, shape, 0).astype(i16)
    return jnp.where(wide == sub, jnp.ones(shape, bf16), jnp.zeros(shape, bf16))


def halo_gather_kernel(send_ref, embeds_ref, out_ref):
    peers, halo = send_ref.shape
    nets = embeds_ref.shape[0]
    for p in range(peers):
        hot = onehot_rows(send_ref[p : p + 1, :], nets)
        out_ref[p * halo : (p + 1) * halo, :] = mm(hot, embeds_ref[...]).astype(bf16)


def adjacency_kernel(neigh_ref, embeds_ref, own_ref, halo_ref, sum_ref):
    degree = neigh_ref.shape[0]
    rows, nets = own_ref.shape
    listed = [neigh_ref[c : c + 1, :] for c in range(degree)]
    columns, counts = [], []
    for c in range(degree):
        count = jnp.ones_like(listed[c])
        seen = None
        for e in range(degree):
            if e != c:
                same = listed[e] == listed[c]
                if e > c:
                    count = count + same.astype(i32)
                else:
                    seen = same if seen is None else (seen | same)
        index = listed[c] if seen is None else jnp.where(seen, -1, listed[c])
        columns.append(column_of(index).astype(i16))
        counts.append(column_of(count).astype(f32).astype(bf16))
    lane = lax.broadcasted_iota(i32, (rows, 128), 1).astype(i16)
    zero = jnp.zeros((rows, 128), bf16)

    def tile(at):
        acc = zero
        here = lane + jnp.int16(at)
        for c in range(degree):
            acc = jnp.where(columns[c] == here, counts[c], acc)
        return acc

    for at in range(0, nets, 128):
        own_ref[:, at : at + 128] = tile(at)
    for at in range(0, halo_ref.shape[1], 128):
        halo_ref[:, at : at + 128] = tile(nets + at)
    sum_ref[...] = mm(own_ref[...], embeds_ref[...])


def layer_kernel(halo_ref, sum_ref, embeds_ref, gnn_ref, received_ref, *refs, degree, far):
    asked_refs, (pre_ref, agg_ref, nets_ref), send_refs = (
        refs[:far],
        refs[far : far + 3],
        refs[far + 3 :],
    )
    nets, feat = nets_ref.shape
    for at in range(0, nets, STEP):
        rows = pl.ds(at, STEP)
        total = sum_ref[rows, :] + mm(halo_ref[rows, :], received_ref[...])
        agg = (total * (1.0 / degree)).astype(bf16)
        agg_ref[rows, :] = agg
        agg_ref.flush(at + STEP)
        pre = mm(embeds_ref[rows, :], gnn_ref[:feat, :]) + mm(agg, gnn_ref[feat:, :])
        pre_ref[rows, :] = pre
        nets_ref[rows, :] = (embeds_ref[rows, :].astype(f32) + gelu_of(pre)).astype(bf16)
    for asked_ref, send_ref in zip(asked_refs, send_refs, strict=True):
        hot = onehot_rows(asked_ref[...], nets)
        send_ref[...] = mm(hot, nets_ref[...]).astype(bf16)


def gather_kernel(nets_ref, *refs):
    some = len(refs) // 2
    for asked_ref, out_ref in zip(refs[:some], refs[some:], strict=True):
        hot = onehot_rows(asked_ref[...], nets_ref.shape[0])
        out_ref[...] = mm(hot, nets_ref[...]).astype(bf16)


def victim_kernel(rid_ref, local_ref, nets_ref, w1_ref, pre_ref, victim_ref, linear_ref, slope_ref):
    regions, slots = local_ref.shape
    nets, feat = nets_ref.shape
    me = rid_ref[0]
    for k in range(regions):
        hot = onehot_rows(local_ref[pl.ds(me ^ k, 1), :], nets)
        victim = mm(hot, nets_ref[...]).astype(bf16)
        victim_ref[k] = victim
        victim_ref.flush(k + 1)
        linear_ref[k] = mm(victim, w1_ref[:feat, :])
    for at in range(0, nets, STEP):
        rows = pl.ds(at, STEP)
        pre = pre_ref[rows, :]
        square = pre * pre
        slope_ref[rows, :] = slope_of(pre, square, gelu_inner(pre, square))
        slope_ref.flush(at + STEP)


def pair_kernel(rid_ref, count_ref, target_ref, linear_ref, w1_ref, w2_ref, *refs, ks, first, last):
    some = len(ks)
    partner_refs, refs = refs[:some], refs[some:]
    if not first:
        before_ref, refs = refs[0], refs[1:]
    lin_grad_ref, sums_ref, *back_refs = refs
    me = rid_ref[0]
    slots, hid = linear_ref.shape[1:]
    feat = partner_refs[0].shape[1]
    w2_row = w2_ref[...].astype(f32)
    w2_column = column_of(w2_row).astype(bf16)
    w2_sum = jnp.zeros((1, hid), f32) if first else before_ref[0:1, :]
    sq_sum = jnp.zeros((1, hid), f32) if first else before_ref[1:2, :]
    slot = lax.broadcasted_iota(i32, (slots, 128), 0)
    for at, k in enumerate(ks):
        linear = linear_ref[k] + mm(partner_refs[at][...], w1_ref[feat:, :])
        square = linear * linear
        inner = gelu_inner(linear, square)
        half = 0.5 * linear
        activated = (half + half * inner).astype(bf16)
        scores = mm(activated, w2_column)
        live = slot < count_ref[0, me ^ k]
        errors = jnp.where(live, scores - column_of(target_ref[pl.ds(me ^ k, 1), :]), 0.0)
        errors = jnp.concatenate([errors] * (hid // 128), 1)
        sq_sum = sq_sum + jnp.sum(errors * errors, 0, keepdims=True)
        residual = 2.0 * errors
        w2_sum = w2_sum + jnp.sum(residual * activated.astype(f32), 0, keepdims=True)
        lin_grad = (residual * w2_row * slope_of(linear, square, inner)).astype(bf16)
        lin_grad_ref[at] = lin_grad
        lin_grad_ref.flush(at + 1)
        back_refs[at][...] = mm_dims(lin_grad, w1_ref[feat:, :], NT).astype(bf16)
    if not last:
        sums_ref[...] = jnp.concatenate([w2_sum, sq_sum, jnp.zeros((6, hid), f32)], 0)
    else:
        count = count_ref[0, 0]
        for q in range(1, count_ref.shape[1]):
            count = count + count_ref[0, q]
        count_row = jnp.zeros((1, hid), f32) + count.astype(f32)
        parts = []
        for row in (w2_sum, sq_sum, count_row):
            high = row.astype(bf16).astype(f32)
            parts += [high, row - high]
        sums_ref[...] = jnp.concatenate(parts + [jnp.zeros((2, hid), f32)], 0)


def w1_grad_kernel(after_ref, victim_ref, sums_ref, *refs, groups):
    regions, _, feat = victim_ref.shape
    partner_refs, lin_refs, out_ref = refs[:regions], refs[regions:-1], refs[-1]
    devices, rows, hid = out_ref.shape
    share = 2 * feat // devices
    top = jnp.zeros((feat, hid), f32)
    low = jnp.zeros((feat, hid), f32)
    for ref, ks in zip(lin_refs, groups, strict=True):
        for at, k in enumerate(ks):
            low = low + mm_dims(partner_refs[k][...], ref[at], TT)
            top = top + mm_dims(victim_ref[k], ref[at], TT)
    both = jnp.concatenate([top, low], 0)
    short = sums_ref[...]
    for d in range(devices):
        out_ref[d] = jnp.concatenate([both[d * share : (d + 1) * share], short], 0).astype(bf16)


def local_grad_kernel(rid_ref, local_ref, w1_ref, *refs, groups, near):
    asked_refs, refs = refs[:near], refs[near:]
    near_refs, refs = refs[:near], refs[near:]
    lin_refs, (grad_ref, vg_ref) = refs[:-2], refs[-2:]
    me = rid_ref[0]
    regions, slots = local_ref.shape
    nets, feat = grad_ref.shape
    for ref, ks in zip(lin_refs, groups, strict=True):
        for at, k in enumerate(ks):
            vg_ref[k * slots : (k + 1) * slots, :] = mm_dims(ref[at], w1_ref[:feat, :], NT).astype(
                bf16
            )
    local = [local_ref[pl.ds(me ^ k, 1), :] for k in range(regions)]
    for at in range(0, nets, BLOCK):
        hot = jnp.concatenate([onehot_cols(row, at, BLOCK) for row in local], 1)
        total = mm(hot, vg_ref[...])
        for k in range(near):
            total = total + mm(onehot_cols(asked_refs[k][...], at, BLOCK), near_refs[k][...])
        grad_ref[at : at + BLOCK, :] = total


def layer_grad_kernel(
    cid_ref, slope_ref, embeds_ref, agg_ref, gnn_ref, halo_ref, grad_ref, *refs, far, peers, degree
):
    asked_refs, refs = refs[:far], refs[far:]
    far_refs, refs = refs[:far], refs[far:]
    (total_ref, pre_grad_ref, agg_grad_ref, gnn_out_ref), refs = refs[:4], refs[4:]
    back_refs, back_ref = refs[:-1], refs[-1]
    nets, feat = grad_ref.shape
    halo = back_refs[0].shape[0]
    top = jnp.zeros((feat, feat), f32)
    low = jnp.zeros((feat, feat), f32)
    for at in range(0, nets, STEP):
        rows = pl.ds(at, STEP)
        total = grad_ref[rows, :]
        for k in range(far):
            total = total + mm(onehot_cols(asked_refs[k][...], at, STEP), far_refs[k][...])
        total_ref[rows, :] = total
        total_ref.flush(at + STEP)
        pre_grad = (total * slope_ref[rows, :]).astype(bf16)
        pre_grad_ref[rows, :] = pre_grad
        pre_grad_ref.flush(at + STEP)
        agg_grad = mm_dims(gnn_ref[feat:, :], pre_grad, NT)
        agg_grad_ref[:, rows] = (agg_grad * (1.0 / degree)).astype(bf16)
        top = top + mm_dims(embeds_ref[rows, :], pre_grad, TT)
        low = low + mm_dims(agg_ref[rows, :], pre_grad, TT)
    agg_grad_ref.flush()
    gnn_out_ref[:feat, :] = top.astype(bf16)
    gnn_out_ref[feat:, :] = low.astype(bf16)
    for at in range(0, halo_ref.shape[1], BLOCK):
        back = mm(agg_grad_ref[...], halo_ref[:, at : at + BLOCK])
        back_ref[at : at + BLOCK, :] = back.T.astype(bf16)
    me = cid_ref[0]
    for k, out_ref in enumerate(back_refs):
        out_ref[...] = back_ref[pl.ds(pl.multiple_of((me ^ k) * halo, halo), halo), :]


def own_grad_kernel(total_ref, pre_grad_ref, gnn_ref, agg_grad_ref, own_ref, out_ref):
    nets, feat = total_ref.shape
    for at in range(0, nets, STEP):
        rows = pl.ds(at, STEP)
        out_ref[rows, :] = (
            total_ref[rows, :]
            + mm_dims(pre_grad_ref[rows, :], gnn_ref[:feat, :], NT)
            + mm(agg_grad_ref[...], own_ref[:, rows]).T
        )


def share_kernel(w1_ref, gnn_ref, *refs, nets_total):
    wide_ref, short_ref = refs[-2:]
    share, hid = gnn_ref.shape[1:]
    w1_sum = jnp.sum(w1_ref[...].astype(f32), 0)
    gnn_sum = jnp.sum(gnn_ref[...].astype(f32), 0)
    short = w1_sum[share:]
    w2_sum = short[0:1] + short[1:2]
    sq_sum = short[2:3] + short[3:4]
    count = short[4:5] + short[5:6]
    factor = 8.0 / jnp.sqrt(count)
    both = (jnp.concatenate([w1_sum[:share], gnn_sum], 0) * factor).astype(bf16)
    wide_ref[...] = jnp.broadcast_to(both[None], wide_ref.shape)
    short_ref[...] = jnp.concatenate(
        [w2_sum * factor, sq_sum / count, 8.0 * nets_total / count, jnp.zeros((5, hid), f32)], 0
    )


def unpack_kernel(spread_ref, w1_ref, gnn_ref):
    devices, rows, _ = spread_ref.shape
    share = rows // 2
    for d in range(devices):
        got = spread_ref[d].astype(f32)
        w1_ref[d * share : (d + 1) * share, :] = got[:share]
        gnn_ref[d * share : (d + 1) * share, :] = got[share:]
        if (d + 1) % (devices // PARTS) == 0:
            w1_ref.flush((d + 1) * share)
            gnn_ref.flush((d + 1) * share)


def final_kernel(cid_ref, short_ref, send_ref, own_ref, *refs):
    got_refs, out_ref = refs[:-1], refs[-1]
    nets = out_ref.shape[0]
    me = cid_ref[0]
    scale = short_ref[2:3, :]
    got = jnp.concatenate([ref[...] for ref in got_refs], 0)
    sent = [send_ref[pl.ds(me ^ k, 1), :] for k in range(len(got_refs))]
    for at in range(0, nets, BLOCK):
        hot = jnp.concatenate([onehot_cols(row, at, BLOCK) for row in sent], 1)
        total = own_ref[at : at + BLOCK, :] + mm(hot, got)
        out_ref[at : at + BLOCK, :] = (total * scale).astype(bf16)


SM = pl.BlockSpec(memory_space=pltpu.SMEM)
VM = pl.BlockSpec(memory_space=pltpu.VMEM)
ANY = pl.BlockSpec(memory_space=pl.ANY)
SMALL = pl.CostEstimate(flops=1, bytes_accessed=1, transcendentals=0)
PARTS = 4


def shape(dims, dtype):
    return jax.ShapeDtypeStruct(dims, dtype)


def in_hbm(dims, dtype):
    return pltpu.MemorySpace.HBM(dims, dtype)


class Load:
    def __init__(self, source, target, sems):
        self.target, self.waited = target, 0
        self.shape = source.shape
        self.rows = max(source.shape[0] // PARTS, 1)
        self.copies = []
        for at in range(source.shape[0] // self.rows):
            part = pl.ds(at * self.rows, self.rows)
            self.copies.append(
                pltpu.make_async_copy(source.at[part], target.at[part], sems.at[at])
            )

    def __getitem__(self, index):
        first = index[0] if isinstance(index, tuple) else index
        last = self.shape[0]
        if isinstance(first, int):
            last = first + 1
        elif isinstance(first, pl.Slice):
            last = first.start + first.size
        while self.waited < -(-last // self.rows):
            self.copies[self.waited].wait()
            self.waited += 1
        return self.target[index]


class Store:
    def __init__(self, source, target, sems):
        self.source, self.target, self.sems = source, target, sems
        self.shape, self.dtype = source.shape, source.dtype
        self.copies, self.sent = [], 0

    def __setitem__(self, index, value):
        self.source[index] = value

    def __getitem__(self, index):
        return self.source[index]

    def flush(self, upto=None):
        upto = self.shape[0] if upto is None else upto
        part = pl.ds(self.sent, upto - self.sent)
        self.copies.append(
            pltpu.make_async_copy(
                self.source.at[part], self.target.at[part], self.sems.at[len(self.copies)]
            )
        )
        self.copies[-1].start()
        self.sent = upto

    def finish(self):
        if self.sent < self.shape[0]:
            self.flush()
        for copy in self.copies:
            copy.wait()


def call(kernel, name, outs, args, scratch=(), mib=24, flops=1):
    ins = [kind for _, kind in args]
    kinds = [kind for _, _, kind in outs]
    staged = [pltpu.VMEM(value.shape, value.dtype) for value, kind in args if kind == "H"]
    staged += [pltpu.VMEM(dims, dtype) for dims, dtype, kind in outs if kind == "H"]
    moved = len(staged)

    def body(*refs):
        operands, refs = list(refs[: len(ins)]), refs[len(ins) :]
        results, refs = list(refs[: len(kinds)]), refs[len(kinds) :]
        buffers, refs = list(refs[:moved]), refs[moved:]
        if moved:
            sems, refs = refs[0], refs[1:]
        at = 0
        for i, kind in enumerate(ins):
            if kind == "H":
                operands[i] = Load(operands[i], buffers[at], sems.at[at])
                at += 1
        loads = [operand for operand in operands if isinstance(operand, Load)]
        for part in range(PARTS):
            for load in loads:
                if part < len(load.copies):
                    load.copies[part].start()
        for i, kind in enumerate(kinds):
            if kind == "H":
                results[i] = Store(buffers[at], results[i], sems.at[at])
                at += 1
        kernel(*operands, *results, *refs)
        for result in results:
            if isinstance(result, Store):
                result.finish()

    spec_of = {"V": VM, "H": ANY, "S": SM, "A": ANY}
    return pl.pallas_call(
        body,
        out_shape=[(in_hbm if kind == "H" else shape)(dims, dtype) for dims, dtype, kind in outs],
        in_specs=[spec_of[kind] for kind in ins],
        out_specs=[spec_of[kind] for kind in kinds],
        scratch_shapes=staged
        + ([pltpu.SemaphoreType.DMA((moved, 2 * PARTS))] if moved else [])
        + list(scratch),
        compiler_params=pltpu.CompilerParams(vmem_limit_bytes=mib << 20),
        cost_estimate=pl.CostEstimate(flops=flops, bytes_accessed=1, transcendentals=0),
        name=name,
    )(
        *[
            pltpu.with_memory_space_constraint(value, pltpu.HBM) if kind == "H" else value
            for value, kind in args
        ]
    )


def exchange(value, axis):
    return lax.all_to_all(value, axis, split_axis=0, concat_axis=0, tiled=True)


def local(
    embeds,
    neighbours,
    halo_send,
    gnn_weight,
    pair_local,
    pair_remote,
    pair_count,
    targets,
    pair_w1,
    pair_w2,
):
    nets, feat = embeds.shape
    hid = pair_w1.shape[1]
    degree = neighbours.shape[1]
    regions, slots = pair_local.shape
    peers, halo = halo_send.shape
    halo_rows = peers * halo
    devices = lax.axis_size("region") * lax.axis_size("dom")
    my_region = lax.axis_index("region").astype(i32)
    rid = my_region.reshape(1)
    cid = lax.axis_index("dom").astype(i32).reshape(1)
    near = 2
    far = regions - near
    share = 2 * feat // devices

    def permute(value, k, axis="region"):
        size = lax.axis_size(axis)
        return lax.ppermute(value, axis, [(i, i ^ k) for i in range(size)])

    def v(*values):
        return [(value, "V") for value in values]

    def h(*values):
        return [(value, "H") for value in values]

    def out(kind, dtype, *dims):
        return [(dims, dtype, kind)]

    (outgoing,) = call(
        halo_gather_kernel,
        "halo_gather",
        out("V", bf16, halo_rows, feat),
        v(halo_send) + h(embeds),
    )
    received = exchange(outgoing.reshape(peers, halo, feat), "dom").reshape(halo_rows, feat)

    wanted = [lax.dynamic_slice_in_dim(pair_remote, my_region ^ k, 1, 0) for k in range(regions)]
    asked = [wanted[0]] + [permute(wanted[k], k) for k in range(1, regions)]

    own, from_halo, agg_sum = pl.pallas_call(
        adjacency_kernel,
        grid=(nets // BLOCK,),
        in_specs=[
            pl.BlockSpec((degree, BLOCK), lambda i: (0, i)),
            pl.BlockSpec((nets, feat), lambda i: (0, 0)),
        ],
        out_specs=[
            pl.BlockSpec((BLOCK, nets), lambda i: (i, 0)),
            pl.BlockSpec((BLOCK, halo_rows), lambda i: (i, 0)),
            pl.BlockSpec((BLOCK, feat), lambda i: (i, 0)),
        ],
        out_shape=[
            in_hbm((nets, nets), bf16),
            in_hbm((nets, halo_rows), bf16),
            in_hbm((nets, feat), f32),
        ],
        compiler_params=pltpu.CompilerParams(vmem_limit_bytes=16 << 20),
        cost_estimate=SMALL,
        name="adjacency",
    )(neighbours.T, embeds)

    pre, aggregate, net_values, *far_sends = call(
        functools.partial(layer_kernel, degree=degree, far=far),
        "layer",
        out("V", f32, nets, feat)
        + out("H", bf16, nets, feat)
        + out("V", bf16, nets, feat)
        + out("V", bf16, slots, feat) * far,
        h(from_halo, agg_sum, embeds, gnn_weight) + v(received, *asked[near:]),
    )
    near_sends = call(
        gather_kernel,
        "gather_near",
        out("V", bf16, slots, feat) * near,
        v(net_values, *asked[:near]),
    )
    partners = [near_sends[0]]
    partners += [permute(near_sends[k], k) for k in range(1, near)]
    partners += [permute(far_sends[k - near], k) for k in range(near, regions)]

    victim, linear_own, slope = call(
        victim_kernel,
        "victims",
        out("H", bf16, regions, slots, feat)
        + out("V", f32, regions, slots, hid)
        + out("H", f32, nets, feat),
        [(rid, "S")] + v(pair_local, net_values) + h(pair_w1) + v(pre),
    )

    groups = [tuple(range(near))] + [(k,) for k in range(near, regions)]
    w2_row = pair_w2.reshape(1, hid)
    lin_grads, backs, sums = [], [], []
    for ks in groups:
        lin_grad, sums_now, *back = call(
            functools.partial(pair_kernel, ks=ks, first=ks is groups[0], last=ks is groups[-1]),
            "pairs",
            out("H", bf16, len(ks), slots, hid)
            + out("V", f32, 8, hid)
            + out("V", bf16, slots, feat) * len(ks),
            [(rid, "S"), (pair_count, "S")]
            + v(targets, linear_own, pair_w1, w2_row)
            + v(*[partners[k] for k in ks])
            + v(*sums),
        )
        lin_grads.append(lin_grad)
        backs += back
        sums = [sums_now]
    returned = [backs[0]] + [permute(backs[k], k) for k in range(1, regions)]

    (local_grad,) = call(
        functools.partial(local_grad_kernel, groups=groups, near=near),
        "local_grads",
        out("V", f32, nets, feat),
        [(rid, "S")]
        + v(pair_local)
        + h(pair_w1)
        + v(*asked[:near], *returned[:near])
        + h(*lin_grads),
        [pltpu.VMEM((regions * slots, feat), bf16)],
    )
    (w1_parts,) = call(
        functools.partial(w1_grad_kernel, groups=groups),
        "w1_grads",
        out("V", bf16, devices, share + 8, hid),
        [(local_grad, "A")] + h(victim) + v(sums[0]) + h(*partners, *lin_grads),
    )
    w1_got = exchange(w1_parts, BOTH)

    total_grad, pre_grad, agg_grad, gnn_part, *backs = call(
        functools.partial(layer_grad_kernel, far=far, peers=peers, degree=degree),
        "layer_grad",
        out("H", f32, nets, feat)
        + out("H", bf16, nets, feat)
        + out("H", bf16, feat, nets)
        + out("V", bf16, 2 * feat, feat)
        + out("V", bf16, halo, feat) * peers,
        [(cid, "S")]
        + h(slope, embeds, aggregate, gnn_weight, from_halo)
        + v(local_grad, *asked[near:], *returned[near:]),
        [pltpu.VMEM((halo_rows, feat), bf16)],
        mib=24,
        flops=10000000000,
    )
    gnn_part, w1_got = lax.optimization_barrier((gnn_part, w1_got))
    gnn_got = exchange(gnn_part.reshape(devices, share, feat), BOTH)
    returned_halo = [backs[0]] + [permute(backs[k], k, "dom") for k in range(1, peers)]

    wide, short = call(
        functools.partial(share_kernel, nets_total=nets * devices),
        "shares",
        out("V", bf16, devices, 2 * share, feat) + out("V", f32, 8, hid),
        v(w1_got, gnn_got) + [(value, "A") for value in returned_halo],
    )
    spread = exchange(wide, BOTH)

    (own_grad,) = call(
        own_grad_kernel,
        "own_grads",
        out("V", f32, nets, feat),
        h(total_grad, pre_grad, gnn_weight, agg_grad, own),
        mib=24,
    )
    (embeds_grad,) = call(
        final_kernel,
        "embeds_grads",
        out("V", bf16, nets, feat),
        [(cid, "S")] + v(short, halo_send, own_grad, *returned_halo),
    )
    w1_grad, gnn_grad = call(
        unpack_kernel,
        "unpack",
        out("H", f32, 2 * feat, hid) + out("H", f32, 2 * feat, feat),
        v(spread),
    )
    return embeds_grad, gnn_grad, w1_grad, short[0], short[1, 0]


def solution(mesh):
    split = P(BOTH, None)
    in_specs = (split, split, split, P(), split, split, split, split, P(), P())
    out_specs = (split, P(), P(), P(), P())
    return jax.shard_map(local, mesh=mesh, in_specs=in_specs, out_specs=out_specs, check_vma=False)
```

```python
import functools
import math

import jax
import jax.numpy as jnp
from jax import lax
from jax.experimental import pallas as pl
from jax.experimental.pallas import tpu as pltpu
from jax.sharding import PartitionSpec as P

bf16 = jnp.bfloat16
f32 = jnp.float32
i32 = jnp.int32
i16 = jnp.int16
gelu_coef = 0.7978845608
BOTH = ("region", "dom")
BLOCK = 256
VICTIMS = 10**10
PAIRS = 2 * 10**9
FINAL = 2 * 10**10
STEP = 512
TT = (((0,), (0,)), ((), ()))
NT = (((1,), (1,)), ((), ()))


def mm(a, b):
    return jnp.dot(a, b, preferred_element_type=f32)


def mm_dims(a, b, dims):
    return lax.dot_general(a, b, dims, preferred_element_type=f32)


def gelu_inner(value, square):
    return jnp.tanh(value * (gelu_coef + (gelu_coef * 0.044715) * square))


def gelu_of(value):
    half = 0.5 * value
    return half + half * gelu_inner(value, value * value)


def slope_of(value, square, inner):
    rise = value * (0.5 * gelu_coef + (1.5 * 0.044715 * gelu_coef) * square)
    return 0.5 + 0.5 * inner + (1.0 - inner * inner) * rise


def column_of(row):
    return jnp.broadcast_to(row, (128, row.shape[1])).T


def onehot_rows(row, width):
    column = column_of(row).astype(i16)
    lane = lax.broadcasted_iota(i32, column.shape, 1).astype(i16)
    one = jnp.ones(column.shape, bf16)
    zero = jnp.zeros(column.shape, bf16)
    return jnp.concatenate(
        [jnp.where(column == lane + jnp.int16(128 * j), one, zero) for j in range(width // 128)], 1
    )


def onehot_cols(row, first, height):
    shape = (height, row.shape[1])
    wide = jnp.broadcast_to(row - first, shape).astype(i16)
    sub = lax.broadcasted_iota(i32, shape, 0).astype(i16)
    return jnp.where(wide == sub, jnp.ones(shape, bf16), jnp.zeros(shape, bf16))


def halo_gather_kernel(send_ref, embeds_ref, out_ref):
    peers, halo = send_ref.shape
    nets = embeds_ref.shape[0]
    for p in range(peers):
        hot = onehot_rows(send_ref[p : p + 1, :], nets)
        out_ref[p * halo : (p + 1) * halo, :] = mm(hot, embeds_ref[...]).astype(bf16)


def adjacency_kernel(neigh_ref, embeds_ref, own_ref, halo_ref, sum_ref, across_ref):
    degree, rows = neigh_ref.shape
    nets, halo_rows = own_ref.shape[1], halo_ref.shape[1]

    @pl.when(pl.program_id(0) == 0)
    def turn():
        across_ref[...] = embeds_ref[...].T

    listed = neigh_ref[...]
    low = listed & 127
    high = listed >> 7
    bit = jnp.left_shift(jnp.ones_like(listed), (high & 7) * 4)
    words = -(-(nets + halo_rows) // 1024)
    parts = [jnp.where((high >> 3) == k, bit, 0) for k in range(words)]
    for first in range(0, 128, 32):
        sub = lax.broadcasted_iota(i32, (32, rows), 0) + first
        packed = [jnp.zeros((32, rows), i32) for _ in range(words)]
        for c in range(degree):
            same = sub == low[c : c + 1, :]
            for k in range(words):
                packed[k] = packed[k] + jnp.where(same, parts[k][c : c + 1, :], 0)
        for at in range(0, nets + halo_rows, 128):
            j = at // 128
            counts = ((packed[j // 8] >> (4 * (j % 8))) & 15).astype(f32).astype(bf16)
            if at < nets:
                own_ref[0, at + first : at + first + 32, :] = counts
            else:
                halo_ref[0, at - nets + first : at - nets + first + 32, :] = counts
    sum_ref[...] = mm(across_ref[...], own_ref[0]).T


def layer_kernel(halo_ref, sum_ref, embeds_ref, gnn_ref, received_ref, *refs, degree, far):
    asked_refs, (pre_ref, agg_ref, nets_ref), send_refs = (
        refs[:far],
        refs[far : far + 3],
        refs[far + 3 :],
    )
    nets, feat = nets_ref.shape
    across = received_ref[...].T
    for at in range(0, nets, STEP):
        rows = pl.ds(at, STEP)
        total = sum_ref[rows, :] + mm(across, halo_ref[at // STEP]).T
        agg = (total * (1.0 / degree)).astype(bf16)
        agg_ref[rows, :] = agg
        agg_ref.flush(at + STEP)
        pre = mm(embeds_ref[rows, :], gnn_ref[:feat, :]) + mm(agg, gnn_ref[feat:, :])
        pre_ref[rows, :] = pre
        nets_ref[rows, :] = (embeds_ref[rows, :].astype(f32) + gelu_of(pre)).astype(bf16)
    for asked_ref, send_ref in zip(asked_refs, send_refs, strict=True):
        hot = onehot_rows(asked_ref[...], nets)
        send_ref[...] = mm(hot, nets_ref[...]).astype(bf16)


def victim_kernel(
    rid_ref, local_ref, nets_ref, w1_ref, pre_ref, *refs, near
):
    asked_refs, (victim_ref, linear_ref, slope_ref), near_refs = (
        refs[:near],
        refs[near : near + 3],
        refs[near + 3 :],
    )
    regions, slots = local_ref.shape
    nets, feat = nets_ref.shape
    me = rid_ref[0]
    for asked_ref, near_ref in zip(asked_refs, near_refs, strict=True):
        hot = onehot_rows(asked_ref[...], nets)
        near_ref[...] = mm(hot, nets_ref[...]).astype(bf16)
    for k in range(regions):
        hot = onehot_rows(local_ref[pl.ds(me ^ k, 1), :], nets)
        victim = mm(hot, nets_ref[...]).astype(bf16)
        victim_ref[k] = victim
        linear_ref[k] = mm(victim, w1_ref[:feat, :])
    victim_ref.flush()
    for at in range(0, nets, STEP):
        rows = pl.ds(at, STEP)
        pre = pre_ref[rows, :]
        square = pre * pre
        slope_ref[rows, :] = slope_of(pre, square, gelu_inner(pre, square)).astype(bf16)
        if at + STEP == nets // 2:
            slope_ref.flush(nets // 2)


def pair_kernel(rid_ref, count_ref, target_ref, linear_ref, w1_ref, w2_ref, *refs, ks, first, last):
    some = len(ks)
    partner_refs, refs = refs[:some], refs[some:]
    if not first:
        before_ref, refs = refs[0], refs[1:]
    lin_grad_ref, sums_ref, *back_refs = refs
    me = rid_ref[0]
    slots, hid = linear_ref.shape[1:]
    feat = partner_refs[0].shape[1]
    w2_row = w2_ref[...].astype(f32)
    w2_column = column_of(w2_row).astype(bf16)
    w2_sum = jnp.zeros((1, hid), f32) if first else before_ref[0:1, :]
    sq_sum = jnp.zeros((1, hid), f32) if first else before_ref[1:2, :]
    slot = lax.broadcasted_iota(i32, (slots, 128), 0)
    for at, k in enumerate(ks):
        linear = linear_ref[k] + mm(partner_refs[at][...], w1_ref[feat:, :])
        square = linear * linear
        inner = gelu_inner(linear, square)
        half = 0.5 * linear
        activated = (half + half * inner).astype(bf16)
        scores = mm(activated, w2_column)
        live = slot < count_ref[0, me ^ k]
        errors = jnp.where(live, scores - column_of(target_ref[pl.ds(me ^ k, 1), :]), 0.0)
        errors = jnp.concatenate([errors] * (hid // 128), 1)
        sq_sum = sq_sum + jnp.sum(errors * errors, 0, keepdims=True)
        residual = 2.0 * errors
        w2_sum = w2_sum + jnp.sum(residual * activated.astype(f32), 0, keepdims=True)
        lin_grad = (residual * w2_row * slope_of(linear, square, inner)).astype(bf16)
        lin_grad_ref[at] = lin_grad
        lin_grad_ref.flush(at + 1)
        back = mm_dims(lin_grad, w1_ref[feat:, :], NT).astype(bf16)
        pieces = len(back_refs) // some
        rows = slots // pieces
        for piece in range(pieces):
            back_refs[at * pieces + piece][...] = back[piece * rows : (piece + 1) * rows]
    if not last:
        sums_ref[...] = jnp.concatenate([w2_sum, sq_sum, jnp.zeros((6, hid), f32)], 0)
    else:
        count = count_ref[0, 0]
        for q in range(1, count_ref.shape[1]):
            count = count + count_ref[0, q]
        count_row = jnp.zeros((1, hid), f32) + count.astype(f32)
        parts = []
        for row in (w2_sum, sq_sum, count_row):
            high = row.astype(bf16).astype(f32)
            parts += [high, row - high]
        sums_ref[...] = jnp.concatenate(parts + [jnp.zeros((2, hid), f32)], 0)


def local_grad_kernel(rid_ref, local_ref, w1_ref, sums_ref, *refs, groups, near):
    regions, slots = local_ref.shape
    asked_refs, refs = refs[:near], refs[near:]
    near_refs, refs = refs[: 2 * near], refs[2 * near :]
    near_rows = [
        jnp.concatenate([near_refs[2 * k][...], near_refs[2 * k + 1][...]], 0) for k in range(near)
    ]
    lin_refs, refs = refs[: len(groups)], refs[len(groups) :]
    partner_refs, (victim_ref, grad_ref, out_ref, vg_ref) = refs[:regions], refs[regions:]
    nets, feat = grad_ref.shape
    devices, _, hid = out_ref.shape
    share = 2 * feat // devices
    me = rid_ref[0]
    lin_grads = {}
    for ref, ks in zip(lin_refs, groups, strict=True):
        for at, k in enumerate(ks):
            lin_grads[k] = ref[at]
            vg_ref[k * slots : (k + 1) * slots, :] = mm_dims(
                lin_grads[k], w1_ref[:feat, :], NT
            ).astype(bf16)
    local = [local_ref[pl.ds(me ^ k, 1), :] for k in range(regions)]
    for at in range(0, nets, BLOCK):
        hot = jnp.concatenate([onehot_cols(row, at, BLOCK) for row in local], 1)
        total = mm(hot, vg_ref[...])
        for k in range(near):
            total = total + mm(onehot_cols(asked_refs[k][...], at, BLOCK), near_rows[k])
        grad_ref[at : at + BLOCK, :] = total
        if (at + BLOCK) * 2 % nets == 0:
            grad_ref.flush(at + BLOCK)
    top = jnp.zeros((feat, hid), f32)
    low = jnp.zeros((feat, hid), f32)
    for k in range(regions):
        top = top + mm_dims(victim_ref[k], lin_grads[k], TT)
        low = low + mm_dims(partner_refs[k][...], lin_grads[k], TT)
    both = jnp.concatenate([top, low], 0)
    short = sums_ref[...]
    for d in range(devices):
        out_ref[d] = jnp.concatenate([both[d * share : (d + 1) * share], short], 0).astype(bf16)


def layer_grad_kernel(
    cid_ref, slope_ref, embeds_ref, agg_ref, gnn_ref, halo_ref, grad_ref, *refs, far, peers, degree
):
    asked_refs, refs = refs[:far], refs[far:]
    far_refs, refs = refs[:far], refs[far:]
    (rest_ref, agg_grad_ref, gnn_out_ref), refs = refs[:3], refs[3:]
    back_refs, back_ref = refs[:-1], refs[-1]
    nets, feat = grad_ref.shape
    halo = back_refs[0].shape[0]
    top = jnp.zeros((feat, feat), f32)
    low = jnp.zeros((feat, feat), f32)
    back = jnp.zeros(back_ref.shape, f32)
    for at in range(0, nets, STEP):
        rows = pl.ds(at, STEP)
        total = grad_ref[rows, :]
        for k in range(far):
            total = total + mm(onehot_cols(asked_refs[k][...], at, STEP), far_refs[k][...])
        pre_grad = (total * slope_ref[rows, :].astype(f32)).astype(bf16)
        agg_grad = mm_dims(pre_grad, gnn_ref[feat:, :], NT)
        agg_grad = (agg_grad * (1.0 / degree)).astype(bf16)
        agg_grad_ref[rows, :] = agg_grad
        rest_ref[rows, :] = total + mm_dims(pre_grad, gnn_ref[:feat, :], NT)
        if (at + STEP) * 2 % nets == 0:
            rest_ref.flush(at + STEP)
            agg_grad_ref.flush(at + STEP)
        top = top + mm_dims(embeds_ref[rows, :], pre_grad, TT)
        low = low + mm_dims(agg_ref[rows, :], pre_grad, TT)
        back = back + mm(halo_ref[at // STEP], agg_grad)
    gnn_out_ref[:feat, :] = top.astype(bf16)
    gnn_out_ref[feat:, :] = low.astype(bf16)
    gnn_out_ref.flush()
    back_ref[...] = back.astype(bf16)
    me = cid_ref[0]
    for k, out_ref in enumerate(back_refs):
        out_ref[...] = back_ref[pl.ds(pl.multiple_of((me ^ k) * halo, halo), halo), :]


def own_grad_kernel(after_ref, rest_ref, agg_grad_ref, own_ref, out_ref):
    nets, feat = out_ref.shape
    for at in range(0, nets, STEP):
        part = mm(own_ref[at // STEP], agg_grad_ref[pl.ds(at, STEP), :])
        if at == 0:
            out_ref[...] = part
        else:
            out_ref[...] += part
    for at in range(0, nets, STEP):
        rows = pl.ds(at, STEP)
        out_ref[rows, :] += rest_ref[rows, :]


def share_kernel(w1_ref, gnn_ref, wide_ref, short_ref, *, nets_total, doms):
    share, hid = gnn_ref.shape[1:]
    w1_sum = jnp.sum(w1_ref[...].astype(f32), 0)
    gnn_sum = jnp.sum(gnn_ref[...].astype(f32), 0)
    short = w1_sum[share:]
    w2_sum = short[0:1] + short[1:2]
    sq_sum = short[2:3] + short[3:4]
    count = short[4:5] + short[5:6]
    factor = 8.0 / jnp.sqrt(count)
    halves = [(w1_sum[:share] * factor).astype(bf16), (gnn_sum * factor).astype(bf16)]
    for d in range(wide_ref.shape[0]):
        wide_ref[d] = halves[d // doms % 2]
    short_ref[...] = jnp.concatenate(
        [w2_sum * factor, sq_sum / count, 8.0 * nets_total / count, jnp.zeros((5, hid), f32)], 0
    )


def unpack_kernel(rid_ref, mine_ref, other_ref, w1_ref, gnn_ref):
    devices, share, _ = mine_ref.shape
    even = rid_ref[0] % 2 == 0
    for d in range(devices):
        rows = slice(d * share, (d + 1) * share)
        mine, other = mine_ref[d].astype(f32), other_ref[d].astype(f32)
        w1_ref[rows, :] = jnp.where(even, mine, other)
        gnn_ref[rows, :] = jnp.where(even, other, mine)
        if (d + 1) % (devices // PARTS) == 0:
            w1_ref.flush((d + 1) * share)
            gnn_ref.flush((d + 1) * share)


def final_kernel(cid_ref, short_ref, send_ref, own_ref, *refs):
    got_refs, (out_ref, w2_ref, loss_ref) = refs[:-3], refs[-3:]
    w2_ref[...] = short_ref[0:1, :]
    loss_ref[...] = short_ref[1:2, :]
    nets = out_ref.shape[0]
    me = cid_ref[0]
    scale = short_ref[2:3, :]
    got = jnp.concatenate([ref[...] for ref in got_refs], 0)
    sent = [send_ref[pl.ds(me ^ k, 1), :] for k in range(len(got_refs))]
    for at in range(0, nets, BLOCK):
        hot = jnp.concatenate([onehot_cols(row, at, BLOCK) for row in sent], 1)
        total = own_ref[at : at + BLOCK, :] + mm(hot, got)
        out_ref[at : at + BLOCK, :] = (total * scale).astype(bf16)


SM = pl.BlockSpec(memory_space=pltpu.SMEM)
VM = pl.BlockSpec(memory_space=pltpu.VMEM)
ANY = pl.BlockSpec(memory_space=pl.ANY)
SMALL = pl.CostEstimate(flops=1, bytes_accessed=1, transcendentals=0)
PARTS = 4


def shape(dims, dtype):
    return jax.ShapeDtypeStruct(dims, dtype)


def in_hbm(dims, dtype):
    return pltpu.MemorySpace.HBM(dims, dtype)


class Load:
    def __init__(self, source, target, sems):
        self.target, self.waited = target, 0
        self.shape = source.shape
        size = math.prod(source.shape) * jnp.dtype(source.dtype).itemsize
        parts = PARTS if size > 1 << 20 else 2 if size > 1 << 19 else 1
        self.rows = max(source.shape[0] // parts, 1)
        self.copies = []
        for at in range(source.shape[0] // self.rows):
            part = pl.ds(at * self.rows, self.rows)
            self.copies.append(
                pltpu.make_async_copy(source.at[part], target.at[part], sems.at[at])
            )

    def __getitem__(self, index):
        first = index[0] if isinstance(index, tuple) else index
        last = self.shape[0]
        if isinstance(first, int):
            last = first + 1
        elif isinstance(first, pl.Slice):
            last = first.start + first.size
        while self.waited < -(-last // self.rows):
            self.copies[self.waited].wait()
            self.waited += 1
        return self.target[index]


class Store:
    def __init__(self, source, target, sems):
        self.source, self.target, self.sems = source, target, sems
        self.shape, self.dtype = source.shape, source.dtype
        self.copies, self.sent = [], 0

    def __setitem__(self, index, value):
        self.source[index] = value

    def __getitem__(self, index):
        return self.source[index]

    def flush(self, upto=None):
        upto = self.shape[0] if upto is None else upto
        part = pl.ds(self.sent, upto - self.sent)
        self.copies.append(
            pltpu.make_async_copy(
                self.source.at[part], self.target.at[part], self.sems.at[len(self.copies)]
            )
        )
        self.copies[-1].start()
        self.sent = upto

    def finish(self):
        if self.sent < self.shape[0]:
            self.flush()
        for copy in self.copies:
            copy.wait()


def call(kernel, name, outs, args, scratch=(), mib=32, flops=1):
    ins = [kind for _, kind in args]
    kinds = [kind for _, _, kind in outs]
    staged = [pltpu.VMEM(value.shape, value.dtype) for value, kind in args if kind == "H"]
    staged += [pltpu.VMEM(dims, dtype) for dims, dtype, kind in outs if kind == "H"]
    moved = len(staged)

    def body(*refs):
        operands, refs = list(refs[: len(ins)]), refs[len(ins) :]
        results, refs = list(refs[: len(kinds)]), refs[len(kinds) :]
        buffers, refs = list(refs[:moved]), refs[moved:]
        if moved:
            sems, refs = refs[0], refs[1:]
        at = 0
        for i, kind in enumerate(ins):
            if kind == "H":
                operands[i] = Load(operands[i], buffers[at], sems.at[at])
                at += 1
        loads = [operand for operand in operands if isinstance(operand, Load)]
        for part in range(PARTS):
            for load in loads:
                if part < len(load.copies):
                    load.copies[part].start()
        for i, kind in enumerate(kinds):
            if kind == "H":
                results[i] = Store(buffers[at], results[i], sems.at[at])
                at += 1
        kernel(*operands, *results, *refs)
        for result in results:
            if isinstance(result, Store):
                result.finish()

    spec_of = {"V": VM, "H": ANY, "S": SM, "A": ANY}
    return pl.pallas_call(
        body,
        out_shape=[(in_hbm if kind == "H" else shape)(dims, dtype) for dims, dtype, kind in outs],
        in_specs=[spec_of[kind] for kind in ins],
        out_specs=[spec_of[kind] for kind in kinds],
        scratch_shapes=staged
        + ([pltpu.SemaphoreType.DMA((moved, 2 * PARTS))] if moved else [])
        + list(scratch),
        compiler_params=pltpu.CompilerParams(vmem_limit_bytes=mib << 20),
        cost_estimate=pl.CostEstimate(flops=flops, bytes_accessed=1, transcendentals=0),
        name=name,
    )(
        *[
            pltpu.with_memory_space_constraint(value, pltpu.HBM) if kind == "H" else value
            for value, kind in args
        ]
    )


def exchange(value, axis):
    return lax.all_to_all(value, axis, split_axis=0, concat_axis=0, tiled=True)


def local(
    embeds,
    neighbours,
    halo_send,
    gnn_weight,
    pair_local,
    pair_remote,
    pair_count,
    targets,
    pair_w1,
    pair_w2,
):
    nets, feat = embeds.shape
    hid = pair_w1.shape[1]
    degree = neighbours.shape[1]
    regions, slots = pair_local.shape
    peers, halo = halo_send.shape
    halo_rows = peers * halo
    devices = lax.axis_size("region") * lax.axis_size("dom")
    my_region = lax.axis_index("region").astype(i32)
    rid = my_region.reshape(1)
    cid = lax.axis_index("dom").astype(i32).reshape(1)
    near = 2
    far = regions - near
    share = 2 * feat // devices

    def permute(value, k, axis="region"):
        size = lax.axis_size(axis)
        return lax.ppermute(value, axis, [(i, i ^ k) for i in range(size)])

    def v(*values):
        return [(value, "V") for value in values]

    def h(*values):
        return [(value, "H") for value in values]

    def out(kind, dtype, *dims):
        return [(dims, dtype, kind)]

    (outgoing,) = call(
        halo_gather_kernel,
        "halo_gather",
        out("V", bf16, halo_rows, feat),
        v(halo_send) + h(embeds),
    )
    received = exchange(outgoing.reshape(peers, halo, feat), "dom").reshape(halo_rows, feat)

    wanted = [lax.dynamic_slice_in_dim(pair_remote, my_region ^ k, 1, 0) for k in range(regions)]
    asked = [wanted[0]] + [permute(wanted[k], k) for k in range(1, regions)]

    steps = nets // STEP
    own, from_halo, agg_sum = pl.pallas_call(
        adjacency_kernel,
        grid=(steps,),
        in_specs=[
            pl.BlockSpec((degree, STEP), lambda i: (0, i)),
            pl.BlockSpec((nets, feat), lambda i: (0, 0)),
        ],
        out_specs=[
            pl.BlockSpec((1, nets, STEP), lambda i: (i, 0, 0)),
            pl.BlockSpec((1, halo_rows, STEP), lambda i: (i, 0, 0)),
            pl.BlockSpec((STEP, feat), lambda i: (i, 0)),
        ],
        out_shape=[
            in_hbm((steps, nets, STEP), bf16),
            in_hbm((steps, halo_rows, STEP), bf16),
            in_hbm((nets, feat), f32),
        ],
        scratch_shapes=[pltpu.VMEM((feat, nets), bf16)],
        compiler_params=pltpu.CompilerParams(vmem_limit_bytes=24 << 20),
        cost_estimate=SMALL,
        name="adjacency",
    )(neighbours.T, embeds)

    pre, aggregate, net_values, *far_sends = call(
        functools.partial(layer_kernel, degree=degree, far=far),
        "layer",
        out("V", f32, nets, feat)
        + out("H", bf16, nets, feat)
        + out("V", bf16, nets, feat)
        + out("V", bf16, slots, feat) * far,
        h(from_halo, agg_sum, embeds, gnn_weight) + v(received, *asked[near:]),
    )
    victim, linear_own, slope, *near_sends = call(
        functools.partial(victim_kernel, near=near),
        "victims",
        out("H", bf16, regions, slots, feat)
        + out("V", f32, regions, slots, hid)
        + out("H", bf16, nets, feat)
        + out("V", bf16, slots, feat) * near,
        [(rid, "S")] + v(pair_local, net_values) + h(pair_w1) + v(pre, *asked[:near]),
        flops=VICTIMS,
    )
    partners = [near_sends[0]]
    partners += [permute(near_sends[k], k) for k in range(1, near)]
    partners += [permute(far_sends[k - near], k) for k in range(near, regions)]

    groups = [(k,) for k in range(near, regions)] + [tuple(range(near))]
    w2_row = pair_w2.reshape(1, hid)
    lin_grads, backs, sums = [], {}, []
    for ks in groups:
        pieces = 2 if ks[0] < near else 1
        lin_grad, sums_now, *back = call(
            functools.partial(pair_kernel, ks=ks, first=ks is groups[0], last=ks is groups[-1]),
            "pairs",
            out("H", bf16, len(ks), slots, hid)
            + out("V", f32, 8, hid)
            + out("V", bf16, slots // pieces, feat) * (pieces * len(ks)),
            [(rid, "S"), (pair_count, "S")]
            + v(targets, linear_own, pair_w1, w2_row)
            + v(*[partners[k] for k in ks])
            + v(*sums),
            flops=PAIRS,
        )
        lin_grads.append(lin_grad)
        for at, k in enumerate(ks):
            backs[k] = back[at * pieces : (at + 1) * pieces]
        sums = [sums_now]
    returned = [backs[0]] + [[permute(x, k) for x in backs[k]] for k in range(1, regions)]

    local_grad, w1_parts = call(
        functools.partial(local_grad_kernel, groups=groups, near=near),
        "local_grads",
        out("H", f32, nets, feat) + out("V", bf16, devices, share + 8, hid),
        [(rid, "S")]
        + v(pair_local)
        + h(pair_w1)
        + v(sums[0], *asked[:near], *sum(returned[:near], []))
        + h(*lin_grads, *partners, victim),
        [pltpu.VMEM((regions * slots, feat), bf16)],
    )
    w1_got = exchange(w1_parts, BOTH)

    rest, agg_grad, gnn_part, *backs = call(
        functools.partial(layer_grad_kernel, far=far, peers=peers, degree=degree),
        "layer_grad",
        out("H", f32, nets, feat)
        + out("H", bf16, nets, feat)
        + out("H", bf16, 2 * feat, feat)
        + out("V", bf16, halo, feat) * peers,
        [(cid, "S")]
        + h(slope, embeds, aggregate, gnn_weight, from_halo, local_grad)
        + v(*asked[near:], *sum(returned[near:], [])),
        [pltpu.VMEM((halo_rows, feat), bf16)],
        flops=10**10,
    )
    gnn_part, w1_got = lax.optimization_barrier((gnn_part, w1_got))
    gnn_got = exchange(gnn_part.reshape(devices, share, feat), BOTH)
    returned_halo = [backs[0]] + [permute(backs[k], k, "dom") for k in range(1, peers)]

    wide, short = call(
        functools.partial(share_kernel, nets_total=nets * devices, doms=peers),
        "shares",
        out("V", bf16, devices, share, feat) + out("V", f32, 8, hid),
        v(w1_got, gnn_got),
    )
    spread = exchange(wide, BOTH)

    (own_grad,) = call(
        own_grad_kernel,
        "own_grads",
        out("V", f32, nets, feat),
        [(short, "A")] + h(rest, agg_grad, own),
    )
    embeds_grad, w2_grad, loss = call(
        final_kernel,
        "embeds_grads",
        out("V", bf16, nets, feat) + out("V", f32, 1, hid) * 2,
        [(cid, "S")] + v(short, halo_send, own_grad, *returned_halo),
        flops=FINAL,
    )
    spread, w2_grad = lax.optimization_barrier((spread, w2_grad))
    w1_grad, gnn_grad = call(
        unpack_kernel,
        "unpack",
        out("H", f32, 2 * feat, hid) + out("H", f32, 2 * feat, feat),
        [(rid, "S")] + v(spread, permute(spread, 1)),
    )
    return embeds_grad, gnn_grad, w1_grad, w2_grad[0], loss[0, 0]


def solution(mesh):
    split = P(BOTH, None)
    in_specs = (split, split, split, P(), split, split, split, split, P(), P())
    out_specs = (split, P(), P(), P(), P())
    return jax.shard_map(local, mesh=mesh, in_specs=in_specs, out_specs=out_specs, check_vma=False)
```

```python
import functools
import math

import jax
import jax.numpy as jnp
from jax import lax
from jax.experimental import pallas as pl
from jax.experimental.pallas import tpu as pltpu
from jax.sharding import PartitionSpec as P

bf16 = jnp.bfloat16
f32 = jnp.float32
i32 = jnp.int32
i16 = jnp.int16
gelu_coef = 0.7978845608
BOTH = ("region", "dom")
BLOCK = 256
VICTIMS = 10**10
PAIRS = 2 * 10**9
LOCAL = 1
SHARES = 1
FINAL = 2 * 10**10
STEP = 512
TT = (((0,), (0,)), ((), ()))
NT = (((1,), (1,)), ((), ()))


def mm(a, b):
    return jnp.dot(a, b, preferred_element_type=f32)


def mm_dims(a, b, dims):
    return lax.dot_general(a, b, dims, preferred_element_type=f32)


def gelu_inner(value, square):
    return jnp.tanh(value * (gelu_coef + (gelu_coef * 0.044715) * square))


def gelu_of(value):
    half = 0.5 * value
    return half + half * gelu_inner(value, value * value)


def slope_of(value, square, inner):
    rise = value * (0.5 * gelu_coef + (1.5 * 0.044715 * gelu_coef) * square)
    return 0.5 + 0.5 * inner + (1.0 - inner * inner) * rise


def column_of(row):
    return jnp.broadcast_to(row, (128, row.shape[1])).T


def onehot_rows(row, width):
    column = column_of(row).astype(i16)
    lane = lax.broadcasted_iota(i32, (16, 128), 1)
    one = jnp.ones(column.shape, bf16)
    zero = jnp.zeros(column.shape, bf16)
    tiles = []
    for j in range(width // 128):
        lanes = jnp.concatenate([(lane + 128 * j).astype(i16)] * (column.shape[0] // 16), 0)
        tiles.append(jnp.where(column == lanes, one, zero))
    return jnp.concatenate(tiles, 1)


def onehot_cols(row, first, height):
    width = row.shape[1]
    wide = jnp.broadcast_to(row, (16, width)).astype(i16)
    wide = jnp.concatenate([wide] * (height // 16), 0)
    sub = (lax.broadcasted_iota(i32, (height, 128), 0) + first).astype(i16)
    sub = jnp.concatenate([sub] * (width // 128), 1)
    return jnp.where(wide == sub, jnp.ones(wide.shape, bf16), jnp.zeros(wide.shape, bf16))


def halo_gather_kernel(send_ref, embeds_ref, out_ref):
    peers, halo = send_ref.shape
    nets = embeds_ref.shape[0]
    group = max(peers // 2, 1)
    sent = send_ref[...]
    hots = [
        jnp.concatenate([onehot_rows(sent[q : q + 1, :], nets) for q in range(p, p + group)], 0)
        for p in range(0, peers, group)
    ]
    for at, hot in enumerate(hots):
        rows = slice(at * group * halo, (at + 1) * group * halo)
        out_ref[rows, :] = mm(hot, embeds_ref[...]).astype(bf16)


def adjacency_kernel(neigh_ref, embeds_ref, own_ref, halo_ref, sum_ref, across_ref):
    degree, rows = neigh_ref.shape
    nets, halo_rows = own_ref.shape[1], halo_ref.shape[1]

    @pl.when(pl.program_id(0) == 0)
    def turn():
        across_ref[...] = embeds_ref[...].T

    listed = neigh_ref[...]
    low = listed & 127
    high = listed >> 7
    bit = jnp.left_shift(jnp.ones_like(listed), (high & 7) * 4)
    words = -(-(nets + halo_rows) // 1024)
    parts = [jnp.where((high >> 3) == k, bit, 0) for k in range(words)]
    for first in range(0, 128, 32):
        sub = lax.broadcasted_iota(i32, (32, rows), 0) + first
        packed = [jnp.zeros((32, rows), i32) for _ in range(words)]
        for c in range(degree):
            same = sub == low[c : c + 1, :]
            for k in range(words):
                packed[k] = packed[k] + jnp.where(same, parts[k][c : c + 1, :], 0)
        for at in range(0, nets + halo_rows, 128):
            j = at // 128
            counts = ((packed[j // 8] >> (4 * (j % 8))) & 15).astype(f32).astype(bf16)
            if at < nets:
                own_ref[0, at + first : at + first + 32, :] = counts
            else:
                halo_ref[0, at - nets + first : at - nets + first + 32, :] = counts
    sum_ref[...] = mm(across_ref[...], own_ref[0]).T


def layer_kernel(halo_ref, sum_ref, embeds_ref, gnn_ref, received_ref, *refs, degree, far):
    asked_refs, (pre_ref, agg_ref, nets_ref), send_refs = (
        refs[:far],
        refs[far : far + 3],
        refs[far + 3 : -1],
    )
    hot_ref = refs[-1]
    nets, feat = nets_ref.shape
    across = received_ref[...].T
    for k, asked_ref in enumerate(asked_refs):
        hot_ref[k] = onehot_rows(asked_ref[...], nets)
    for at in range(0, nets, STEP):
        rows = pl.ds(at, STEP)
        total = sum_ref[rows, :] + mm(across, halo_ref[at // STEP]).T
        agg = (total * (1.0 / degree)).astype(bf16)
        agg_ref[rows, :] = agg
        agg_ref.flush(at + STEP)
        pre = mm(embeds_ref[rows, :], gnn_ref[:feat, :]) + mm(agg, gnn_ref[feat:, :])
        pre_ref[rows, :] = pre
        nets_ref[rows, :] = (embeds_ref[rows, :].astype(f32) + gelu_of(pre)).astype(bf16)
    for k, send_ref in enumerate(send_refs):
        send_ref[...] = mm(hot_ref[k], nets_ref[...]).astype(bf16)


def victim_kernel(
    rid_ref, local_ref, nets_ref, w1_ref, pre_ref, *refs, near
):
    asked_refs, (victim_ref, linear_ref, slope_ref), near_refs = (
        refs[:near],
        refs[near : near + 3],
        refs[near + 3 :],
    )
    regions, slots = local_ref.shape
    nets, feat = nets_ref.shape
    me = rid_ref[0]
    for at in range(0, nets, STEP):
        rows = pl.ds(at, STEP)
        pre = pre_ref[rows, :]
        square = pre * pre
        slope_ref[rows, :] = slope_of(pre, square, gelu_inner(pre, square)).astype(bf16)
    slope_ref.flush()
    for k in range(regions):
        hot = onehot_rows(local_ref[pl.ds(me ^ k, 1), :], nets)
        victim_ref[k] = mm(hot, nets_ref[...]).astype(bf16)
    victim_ref.flush()
    for asked_ref, near_ref in zip(asked_refs, near_refs, strict=True):
        hot = onehot_rows(asked_ref[...], nets)
        near_ref[...] = mm(hot, nets_ref[...]).astype(bf16)
    for k in range(regions):
        linear_ref[k] = mm(victim_ref[k], w1_ref[:feat, :])


def pair_kernel(rid_ref, count_ref, target_ref, linear_ref, w1_ref, w2_ref, *refs, ks, first, last):
    some = len(ks)
    slots, hid = linear_ref.shape[1:]
    feat = refs[0].shape[1]
    me = rid_ref[0]
    partner_refs, refs = refs[:some], refs[some:]
    if last:
        victim_ref, refs = refs[0], refs[1:]
        others = victim_ref.shape[0] - some
        old_partner_refs, old_lin_ref, refs = refs[:others], refs[others], refs[others + 1 :]
    if not first:
        before_ref, refs = refs[0], refs[1:]
    lin_grad_ref, sums_ref, *back_refs = refs
    across = []
    w2_row = w2_ref[...].astype(f32)
    w2_column = column_of(w2_row).astype(bf16)
    w2_sum = jnp.zeros((1, hid), f32) if first else before_ref[0:1, :]
    sq_sum = jnp.zeros((1, hid), f32) if first else before_ref[1:2, :]
    slot = lax.broadcasted_iota(i32, (slots, 128), 0)
    for at, k in enumerate(ks):
        linear = linear_ref[k] + mm(partner_refs[at][...], w1_ref[feat:, :])
        square = linear * linear
        inner = gelu_inner(linear, square)
        half = 0.5 * linear
        activated = (half + half * inner).astype(bf16)
        scores = mm(activated, w2_column)
        live = slot < count_ref[0, me ^ k]
        errors = jnp.where(live, scores - column_of(target_ref[pl.ds(me ^ k, 1), :]), 0.0)
        errors = jnp.concatenate([errors] * (hid // 128), 1)
        sq_sum = sq_sum + jnp.sum(errors * errors, 0, keepdims=True)
        residual = 2.0 * errors
        w2_sum = w2_sum + jnp.sum(residual * activated.astype(f32), 0, keepdims=True)
        lin_grad = (residual * w2_row * slope_of(linear, square, inner)).astype(bf16)
        lin_grad_ref[at] = lin_grad
        lin_grad_ref.flush(at + 1)
        back = mm_dims(lin_grad, w1_ref[feat:, :], NT).astype(bf16)
        pieces = len(back_refs) // some
        rows = slots // pieces
        for piece in range(pieces):
            back_refs[at * pieces + piece][...] = back[piece * rows : (piece + 1) * rows]
        if last:
            across.append(lin_grad.T)
    if not last:
        sums_ref[...] = jnp.concatenate([w2_sum, sq_sum, jnp.zeros((6, hid), f32)], 0)
        return
    for at in range(others):
        across.append(old_lin_ref[at].T)
    across = jnp.concatenate(across, 1)
    victims = jnp.concatenate([victim_ref[k] for k in range(some + others)], 0)
    partners = jnp.concatenate([ref[...] for ref in [*partner_refs, *old_partner_refs]], 0)
    both = jnp.concatenate([mm(across, victims).T, mm(across, partners).T], 0)
    count = count_ref[0, 0]
    for q in range(1, count_ref.shape[1]):
        count = count + count_ref[0, q]
    count_row = jnp.zeros((1, hid), f32) + count.astype(f32)
    parts = []
    for row in (w2_sum, sq_sum, count_row):
        high = row.astype(bf16).astype(f32)
        parts += [high, row - high]
    short = jnp.concatenate(parts + [jnp.zeros((2, hid), f32)], 0)
    devices = sums_ref.shape[0]
    share = 2 * feat // devices
    for d in range(devices):
        sums_ref[d] = jnp.concatenate([both[d * share : (d + 1) * share], short], 0).astype(bf16)


def local_grad_kernel(rid_ref, local_ref, w1_ref, after_ref, *refs, groups, near):
    regions, slots = local_ref.shape
    asked_refs, refs = refs[:near], refs[near:]
    near_refs, refs = refs[: 2 * near], refs[2 * near :]
    lin_refs, (grad_ref, vg_ref) = refs[: len(groups)], refs[len(groups) :]
    nets, feat = grad_ref.shape
    me = rid_ref[0]
    returned = jnp.concatenate([near_ref[...] for near_ref in near_refs], 0)
    for at in range(0, nets, BLOCK):
        hot = jnp.concatenate([onehot_cols(ref[...], at, BLOCK) for ref in asked_refs], 1)
        grad_ref[at : at + BLOCK, :] = mm(hot, returned)
    for ref, ks in zip(lin_refs, groups, strict=True):
        for at, k in enumerate(ks):
            vg_ref[k * slots : (k + 1) * slots, :] = mm_dims(ref[at], w1_ref[:feat, :], NT).astype(
                bf16
            )
    listed = [local_ref[pl.ds(me ^ k, 1), :] for k in range(regions)]
    for at in range(0, nets, BLOCK):
        hot = jnp.concatenate([onehot_cols(row, at, BLOCK) for row in listed], 1)
        grad_ref[at : at + BLOCK, :] += mm(hot, vg_ref[...])
        if (at + BLOCK) * PARTS % nets == 0:
            grad_ref.flush(at + BLOCK)


def layer_grad_kernel(
    cid_ref, grad_ref, slope_ref, gnn_ref, embeds_ref, agg_ref, halo_ref, *refs, far, peers, degree
):
    asked_refs, refs = refs[:far], refs[far:]
    far_refs, refs = refs[:far], refs[far:]
    (rest_ref, agg_grad_ref, gnn_out_ref), refs = refs[:3], refs[3:]
    back_refs, back_ref = refs[:-1], refs[-1]
    nets, feat = grad_ref.shape
    halo = back_refs[0].shape[0]
    top = jnp.zeros((feat, feat), f32)
    low = jnp.zeros((feat, feat), f32)
    returned = jnp.concatenate([ref[...] for ref in far_refs], 0)
    for at in range(0, nets, STEP):
        rows = pl.ds(at, STEP)
        hot = jnp.concatenate([onehot_cols(ref[...], at, STEP) for ref in asked_refs], 1)
        total = mm(hot, returned)
        total = total + grad_ref[rows, :]
        pre_grad = (total * slope_ref[rows, :].astype(f32)).astype(bf16)
        agg_grad = mm_dims(pre_grad, gnn_ref[feat:, :], NT)
        agg_grad = (agg_grad * (1.0 / degree)).astype(bf16)
        agg_grad_ref[rows, :] = agg_grad
        rest_ref[rows, :] = (total + mm_dims(pre_grad, gnn_ref[:feat, :], NT)).astype(bf16)
        if (at + STEP) * 2 % nets == 0:
            rest_ref.flush(at + STEP)
            agg_grad_ref.flush(at + STEP)
        top = top + mm_dims(embeds_ref[rows, :], pre_grad, TT)
        low = low + mm_dims(agg_ref[rows, :], pre_grad, TT)
    gnn_out_ref[:feat, :] = top.astype(bf16)
    gnn_out_ref[feat:, :] = low.astype(bf16)
    gnn_out_ref.flush()
    back = jnp.zeros(back_ref.shape, f32)
    for at in range(0, nets, STEP):
        back = back + mm(halo_ref[at // STEP], agg_grad_ref[pl.ds(at, STEP), :])
    back_ref[...] = back.astype(bf16)
    me = cid_ref[0]
    for k, out_ref in enumerate(back_refs):
        out_ref[...] = back_ref[pl.ds(pl.multiple_of((me ^ k) * halo, halo), halo), :]


def share_kernel(w1_ref, gnn_ref, wide_ref, short_ref, *, nets_total, doms):
    share, hid = gnn_ref.shape[1:]
    w1_sum = jnp.sum(w1_ref[...].astype(f32), 0)
    gnn_sum = jnp.sum(gnn_ref[...].astype(f32), 0)
    short = w1_sum[share:]
    w2_sum = short[0:1] + short[1:2]
    sq_sum = short[2:3] + short[3:4]
    count = short[4:5] + short[5:6]
    factor = 8.0 / jnp.sqrt(count)
    halves = [(w1_sum[:share] * factor).astype(bf16), (gnn_sum * factor).astype(bf16)]
    for d in range(wide_ref.shape[0]):
        wide_ref[d] = halves[d // doms % 2]
    short_ref[...] = jnp.concatenate(
        [w2_sum * factor, sq_sum / count, 8.0 * nets_total / count, jnp.zeros((5, hid), f32)], 0
    )


def unpack_kernel(rid_ref, mine_ref, other_ref, w1_ref, gnn_ref):
    devices, share, _ = mine_ref.shape
    even = rid_ref[0] % 2 == 0
    for d in range(devices):
        rows = slice(d * share, (d + 1) * share)
        mine, other = mine_ref[d].astype(f32), other_ref[d].astype(f32)
        w1_ref[rows, :] = jnp.where(even, mine, other)
        gnn_ref[rows, :] = jnp.where(even, other, mine)
        if (d + 1) % (devices // PARTS) == 0:
            w1_ref.flush((d + 1) * share)
            gnn_ref.flush((d + 1) * share)


def final_kernel(cid_ref, short_ref, send_ref, rest_ref, agg_grad_ref, own_ref, *refs):
    got_refs, (out_ref, w2_ref, loss_ref, given_ref) = refs[:-4], refs[-4:]
    w2_ref[...] = short_ref[0:1, :]
    loss_ref[...] = short_ref[1:2, :]
    nets = out_ref.shape[0]
    me = cid_ref[0]
    scale = short_ref[2:3, :]
    got = jnp.concatenate([ref[...] for ref in got_refs], 0)
    sent = [send_ref[pl.ds(me ^ k, 1), :] for k in range(len(got_refs))]
    given_ref[: got.shape[0], :] = got
    hots = [
        jnp.concatenate([onehot_cols(row, at, BLOCK) for row in sent], 1)
        for at in range(0, nets, BLOCK)
    ]
    given_ref[got.shape[0] :, :] = agg_grad_ref[...]
    for at in range(0, nets, BLOCK):
        rows = pl.ds(at, BLOCK)
        parts = [own_ref[i, rows, :] for i in range(own_ref.shape[0])]
        total = mm(jnp.concatenate([hots[at // BLOCK]] + parts, 1), given_ref[...])
        out_ref[rows, :] = ((total + rest_ref[rows, :]) * scale).astype(bf16)
        if (at + BLOCK) * PARTS % nets == 0:
            out_ref.flush(at + BLOCK)


SM = pl.BlockSpec(memory_space=pltpu.SMEM)
VM = pl.BlockSpec(memory_space=pltpu.VMEM)
ANY = pl.BlockSpec(memory_space=pl.ANY)
SMALL = pl.CostEstimate(flops=1, bytes_accessed=1, transcendentals=0)
PARTS = 4


def shape(dims, dtype):
    return jax.ShapeDtypeStruct(dims, dtype)


def in_hbm(dims, dtype):
    return pltpu.MemorySpace.HBM(dims, dtype)


class Load:
    def __init__(self, source, target, sem):
        self.target, self.shape, self.waited = target, source.shape, False
        self.copy = pltpu.make_async_copy(source, target, sem)
        self.copy.start()

    def wait(self):
        if not self.waited:
            self.copy.wait()
        self.waited = True

    def __getitem__(self, index):
        self.wait()
        return self.target[index]


class Store:
    def __init__(self, source, target, sems):
        self.source, self.target, self.sems = source, target, sems
        self.shape, self.dtype = source.shape, source.dtype
        self.copies, self.sent = [], 0

    def __setitem__(self, index, value):
        self.source[index] = value

    def __getitem__(self, index):
        return self.source[index]

    def flush(self, upto=None):
        upto = self.shape[0] if upto is None else upto
        part = pl.ds(self.sent, upto - self.sent)
        self.copies.append(
            pltpu.make_async_copy(
                self.source.at[part], self.target.at[part], self.sems.at[len(self.copies)]
            )
        )
        self.copies[-1].start()
        self.sent = upto

    def finish(self):
        if self.sent < self.shape[0]:
            self.flush()
        for copy in self.copies:
            copy.wait()


def call(kernel, name, outs, args, scratch=(), mib=32, flops=1):
    ins = [kind for _, kind in args]
    kinds = [kind for _, _, kind in outs]
    staged = [pltpu.VMEM(value.shape, value.dtype) for value, kind in args if kind == "H"]
    staged += [pltpu.VMEM(dims, dtype) for dims, dtype, kind in outs if kind == "H"]
    moved = len(staged)

    def body(*refs):
        operands, refs = list(refs[: len(ins)]), refs[len(ins) :]
        results, refs = list(refs[: len(kinds)]), refs[len(kinds) :]
        buffers, refs = list(refs[:moved]), refs[moved:]
        if moved:
            sems, refs = refs[0], refs[1:]
        at = 0
        for i, kind in enumerate(ins):
            if kind == "H":
                operands[i] = Load(operands[i], buffers[at], sems.at[at, 0])
                at += 1
        for i, kind in enumerate(kinds):
            if kind == "H":
                results[i] = Store(buffers[at], results[i], sems.at[at])
                at += 1
        kernel(*operands, *results, *refs)
        for operand in operands:
            if isinstance(operand, Load):
                operand.wait()
        for result in results:
            if isinstance(result, Store):
                result.finish()

    spec_of = {"V": VM, "H": ANY, "S": SM, "A": ANY}
    return pl.pallas_call(
        body,
        out_shape=[(in_hbm if kind == "H" else shape)(dims, dtype) for dims, dtype, kind in outs],
        in_specs=[spec_of[kind] for kind in ins],
        out_specs=[spec_of[kind] for kind in kinds],
        scratch_shapes=staged
        + ([pltpu.SemaphoreType.DMA((moved, 2 * PARTS))] if moved else [])
        + list(scratch),
        compiler_params=pltpu.CompilerParams(vmem_limit_bytes=mib << 20),
        cost_estimate=pl.CostEstimate(flops=flops, bytes_accessed=1, transcendentals=0),
        name=name,
    )(
        *[
            pltpu.with_memory_space_constraint(value, pltpu.HBM) if kind == "H" else value
            for value, kind in args
        ]
    )


def exchange(value, axis):
    return lax.all_to_all(value, axis, split_axis=0, concat_axis=0, tiled=True)


def local(
    embeds,
    neighbours,
    halo_send,
    gnn_weight,
    pair_local,
    pair_remote,
    pair_count,
    targets,
    pair_w1,
    pair_w2,
):
    nets, feat = embeds.shape
    hid = pair_w1.shape[1]
    degree = neighbours.shape[1]
    regions, slots = pair_local.shape
    peers, halo = halo_send.shape
    halo_rows = peers * halo
    devices = lax.axis_size("region") * lax.axis_size("dom")
    my_region = lax.axis_index("region").astype(i32)
    rid = my_region.reshape(1)
    cid = lax.axis_index("dom").astype(i32).reshape(1)
    near = 2
    far = regions - near
    share = 2 * feat // devices

    def permute(value, k, axis="region"):
        size = lax.axis_size(axis)
        return lax.ppermute(value, axis, [(i, i ^ k) for i in range(size)])

    def v(*values):
        return [(value, "V") for value in values]

    def h(*values):
        return [(value, "H") for value in values]

    def out(kind, dtype, *dims):
        return [(dims, dtype, kind)]

    (outgoing,) = call(
        halo_gather_kernel,
        "halo_gather",
        out("V", bf16, halo_rows, feat),
        h(halo_send, embeds),
    )
    received = exchange(outgoing.reshape(peers, halo, feat), "dom").reshape(halo_rows, feat)

    wanted = [lax.dynamic_slice_in_dim(pair_remote, my_region ^ k, 1, 0) for k in range(regions)]
    asked = [wanted[0]] + [permute(wanted[k], k) for k in range(1, regions)]

    steps = nets // STEP
    own, from_halo, agg_sum = pl.pallas_call(
        adjacency_kernel,
        grid=(steps,),
        in_specs=[
            pl.BlockSpec((degree, STEP), lambda i: (0, i)),
            pl.BlockSpec((nets, feat), lambda i: (0, 0)),
        ],
        out_specs=[
            pl.BlockSpec((1, nets, STEP), lambda i: (i, 0, 0)),
            pl.BlockSpec((1, halo_rows, STEP), lambda i: (i, 0, 0)),
            pl.BlockSpec((STEP, feat), lambda i: (i, 0)),
        ],
        out_shape=[
            in_hbm((steps, nets, STEP), bf16),
            in_hbm((steps, halo_rows, STEP), bf16),
            in_hbm((nets, feat), f32),
        ],
        scratch_shapes=[pltpu.VMEM((feat, nets), bf16)],
        compiler_params=pltpu.CompilerParams(vmem_limit_bytes=24 << 20),
        cost_estimate=SMALL,
        name="adjacency",
    )(neighbours.T, embeds)

    pre, aggregate, net_values, *far_sends = call(
        functools.partial(layer_kernel, degree=degree, far=far),
        "layer",
        out("V", f32, nets, feat)
        + out("H", bf16, nets, feat)
        + out("V", bf16, nets, feat)
        + out("V", bf16, slots, feat) * far,
        h(from_halo, agg_sum) + v(embeds, gnn_weight, received, *asked[near:]),
        [pltpu.VMEM((far, slots, nets), bf16)],
    )
    victim, linear_own, slope, *near_sends = call(
        functools.partial(victim_kernel, near=near),
        "victims",
        out("H", bf16, regions, slots, feat)
        + out("V", f32, regions, slots, hid)
        + out("H", bf16, nets, feat)
        + out("V", bf16, slots, feat) * near,
        [(rid, "S")] + v(pair_local, net_values) + h(pair_w1) + v(pre, *asked[:near]),
        flops=VICTIMS,
    )
    partners = [near_sends[0]]
    partners += [permute(near_sends[k], k) for k in range(1, near)]
    partners += [permute(far_sends[k - near], k) for k in range(near, regions)]

    groups = [tuple(range(near, regions)), tuple(range(near))]
    w2_row = pair_w2.reshape(1, hid)
    lin_grads, backs, sums = [], {}, []
    for ks in groups:
        last = ks is groups[-1]
        pieces = 2 if last else 1
        lin_grad, sums_now, *back = call(
            functools.partial(pair_kernel, ks=ks, first=ks is groups[0], last=last),
            "pairs",
            out("H", bf16, len(ks), slots, hid)
            + (out("V", bf16, devices, share + 8, hid) if last else out("V", f32, 8, hid))
            + out("V", bf16, slots // pieces, feat) * (pieces * len(ks)),
            [(rid, "S"), (pair_count, "S")]
            + v(targets, linear_own, pair_w1, w2_row)
            + v(*[partners[k] for k in ks])
            + (h(victim, *partners[near:], *lin_grads) if last else [])
            + v(*sums),
            flops=PAIRS,
        )
        lin_grads.append(lin_grad)
        for at, k in enumerate(ks):
            backs[k] = back[at * pieces : (at + 1) * pieces]
        sums = [sums_now]
    returned = [backs[0]] + [[permute(x, k) for x in backs[k]] for k in range(1, regions)]

    (w1_parts,) = sums
    w1_got = exchange(w1_parts, BOTH)
    (local_grad,) = call(
        functools.partial(local_grad_kernel, groups=groups, near=near),
        "local_grads",
        out("H", f32, nets, feat),
        [(rid, "S")]
        + v(pair_local)
        + h(pair_w1)
        + [(w1_parts, "A")]
        + v(*asked[:near], *sum(returned[:near], []))
        + h(*lin_grads),
        [pltpu.VMEM((regions * slots, feat), bf16)],
        flops=LOCAL,
    )
    rest, agg_grad, gnn_part, *backs = call(
        functools.partial(layer_grad_kernel, far=far, peers=peers, degree=degree),
        "layer_grad",
        out("H", bf16, nets, feat) * 2
        + out("H", bf16, 2 * feat, feat)
        + out("V", bf16, halo, feat) * peers,
        [(cid, "S")]
        + h(local_grad, slope)
        + v(gnn_weight, embeds)
        + h(aggregate, from_halo)
        + v(*asked[near:], *sum(returned[near:], [])),
        [pltpu.VMEM((halo_rows, feat), bf16)],
        flops=10**10,
    )
    gnn_part, w1_got = lax.optimization_barrier((gnn_part, w1_got))
    gnn_got = exchange(gnn_part.reshape(devices, share, feat), BOTH)
    returned_halo = {k: permute(backs[k], k, "dom") for k in range(peers - 1, 0, -1)}
    returned_halo = [backs[0]] + [returned_halo[k] for k in range(1, peers)]

    wide, short = call(
        functools.partial(share_kernel, nets_total=nets * devices, doms=peers),
        "shares",
        out("V", bf16, devices, share, feat) + out("V", f32, 8, hid),
        v(w1_got, gnn_got),
        flops=SHARES,
    )
    spread = exchange(wide, BOTH)

    embeds_grad, w2_grad, loss = call(
        final_kernel,
        "embeds_grads",
        out("H", bf16, nets, feat) + out("V", f32, 1, hid) * 2,
        [(cid, "S")] + v(short, halo_send) + h(rest, agg_grad, own) + v(*returned_halo),
        [pltpu.VMEM((halo_rows + nets, feat), bf16)],
        flops=FINAL,
    )
    spread, w2_grad = lax.optimization_barrier((spread, w2_grad))
    w1_grad, gnn_grad = call(
        unpack_kernel,
        "unpack",
        out("H", f32, 2 * feat, hid) + out("H", f32, 2 * feat, feat),
        [(rid, "S")] + v(spread, permute(spread, 1)),
    )
    return embeds_grad, gnn_grad, w1_grad, w2_grad[0], loss[0, 0]


def solution(mesh):
    split = P(BOTH, None)
    in_specs = (split, split, split, P(), split, split, split, split, P(), P())
    out_specs = (split, P(), P(), P(), P())
    return jax.shard_map(local, mesh=mesh, in_specs=in_specs, out_specs=out_specs, check_vma=False)
```

```python
import functools
import math

import jax
import jax.numpy as jnp
from jax import lax
from jax.experimental import pallas as pl
from jax.experimental.pallas import tpu as pltpu
from jax.sharding import PartitionSpec as P

bf16 = jnp.bfloat16
f32 = jnp.float32
i32 = jnp.int32
i16 = jnp.int16
gelu_coef = 0.7978845608
BOTH = ("region", "dom")
BLOCK = 256
VICTIMS = 10**10
PAIRS = 2 * 10**9
LOCAL = 1
SHARES = 1
FINAL = 2 * 10**10
STEP = 512
TT = (((0,), (0,)), ((), ()))
NT = (((1,), (1,)), ((), ()))


def mm(a, b):
    return jnp.dot(a, b, preferred_element_type=f32)


def mm_dims(a, b, dims):
    return lax.dot_general(a, b, dims, preferred_element_type=f32)


def gelu_inner(value, square):
    return jnp.tanh(value * (gelu_coef + (gelu_coef * 0.044715) * square))


def gelu_of(value):
    half = 0.5 * value
    return half + half * gelu_inner(value, value * value)


def slope_of(value, square, inner):
    rise = value * (0.5 * gelu_coef + (1.5 * 0.044715 * gelu_coef) * square)
    return 0.5 + 0.5 * inner + (1.0 - inner * inner) * rise


def column_of(row):
    return jnp.broadcast_to(row, (128, row.shape[1])).T


def onehot_rows(row, width):
    column = column_of(row).astype(i16)
    lane = lax.broadcasted_iota(i32, (16, 128), 1)
    one = jnp.ones(column.shape, bf16)
    zero = jnp.zeros(column.shape, bf16)
    tiles = []
    for j in range(width // 128):
        lanes = jnp.concatenate([(lane + 128 * j).astype(i16)] * (column.shape[0] // 16), 0)
        tiles.append(jnp.where(column == lanes, one, zero))
    return jnp.concatenate(tiles, 1)


def onehot_cols(row, first, height):
    width = row.shape[1]
    wide = jnp.broadcast_to(row, (16, width)).astype(i16)
    wide = jnp.concatenate([wide] * (height // 16), 0)
    sub = (lax.broadcasted_iota(i32, (height, 128), 0) + first).astype(i16)
    sub = jnp.concatenate([sub] * (width // 128), 1)
    return jnp.where(wide == sub, jnp.ones(wide.shape, bf16), jnp.zeros(wide.shape, bf16))


def halo_gather_kernel(send_ref, embeds_ref, out_ref):
    peers, halo = send_ref.shape
    nets = embeds_ref.shape[0]
    group = max(peers // 2, 1)
    sent = send_ref[...]
    hots = [
        jnp.concatenate([onehot_rows(sent[q : q + 1, :], nets) for q in range(p, p + group)], 0)
        for p in range(0, peers, group)
    ]
    for at, hot in enumerate(hots):
        rows = slice(at * group * halo, (at + 1) * group * halo)
        out_ref[rows, :] = mm(hot, embeds_ref[...]).astype(bf16)


def adjacency_kernel(neigh_ref, embeds_ref, own_ref, halo_ref, sum_ref, across_ref):
    degree, rows = neigh_ref.shape
    nets, halo_rows = own_ref.shape[1], halo_ref.shape[1]

    @pl.when(pl.program_id(0) == 0)
    def turn():
        across_ref[...] = embeds_ref[...].T

    listed = neigh_ref[...]
    low = listed & 127
    high = listed >> 7
    bit = jnp.left_shift(jnp.ones_like(listed), (high & 7) * 4)
    words = -(-(nets + halo_rows) // 1024)
    parts = [jnp.where((high >> 3) == k, bit, 0) for k in range(words)]
    for first in range(0, 128, 32):
        sub = lax.broadcasted_iota(i32, (32, rows), 0) + first
        packed = [jnp.zeros((32, rows), i32) for _ in range(words)]
        for c in range(degree):
            same = sub == low[c : c + 1, :]
            for k in range(words):
                packed[k] = packed[k] + jnp.where(same, parts[k][c : c + 1, :], 0)
        for at in range(0, nets + halo_rows, 128):
            j = at // 128
            counts = ((packed[j // 8] >> (4 * (j % 8))) & 15).astype(f32).astype(bf16)
            if at < nets:
                own_ref[0, at + first : at + first + 32, :] = counts
            else:
                halo_ref[0, at - nets + first : at - nets + first + 32, :] = counts
    sum_ref[...] = mm(across_ref[...], own_ref[0]).T


def layer_kernel(halo_ref, sum_ref, embeds_ref, gnn_ref, received_ref, *refs, degree, far):
    asked_refs, (pre_ref, agg_ref, nets_ref), send_refs = (
        refs[:far],
        refs[far : far + 3],
        refs[far + 3 : -1],
    )
    hot_ref = refs[-1]
    nets, feat = nets_ref.shape
    across = received_ref[...].T
    for k, asked_ref in enumerate(asked_refs):
        hot_ref[k] = onehot_rows(asked_ref[...], nets)
    for at in range(0, nets, STEP):
        rows = pl.ds(at, STEP)
        pre_ref[rows, :] = mm(embeds_ref[rows, :], gnn_ref[:feat, :])
    for at in range(0, nets, STEP):
        rows = pl.ds(at, STEP)
        total = mm(across, halo_ref[at // STEP]).T
        total = total + sum_ref[rows, :]
        agg = (total * (1.0 / degree)).astype(bf16)
        agg_ref[rows, :] = agg
        agg_ref.flush(at + STEP)
        pre = pre_ref[rows, :] + mm(agg, gnn_ref[feat:, :])
        pre_ref[rows, :] = pre
        nets_ref[rows, :] = (embeds_ref[rows, :].astype(f32) + gelu_of(pre)).astype(bf16)
    for k, send_ref in enumerate(send_refs):
        send_ref[...] = mm(hot_ref[k], nets_ref[...]).astype(bf16)


def victim_kernel(
    rid_ref, local_ref, nets_ref, w1_ref, pre_ref, *refs, near
):
    asked_refs, (victim_ref, linear_ref, slope_ref), near_refs = (
        refs[:near],
        refs[near : near + 3],
        refs[near + 3 :],
    )
    regions, slots = local_ref.shape
    nets, feat = nets_ref.shape
    me = rid_ref[0]
    for at in range(0, nets, STEP):
        rows = pl.ds(at, STEP)
        pre = pre_ref[rows, :]
        square = pre * pre
        slope_ref[rows, :] = slope_of(pre, square, gelu_inner(pre, square)).astype(bf16)
    slope_ref.flush()
    for k in range(regions):
        hot = onehot_rows(local_ref[pl.ds(me ^ k, 1), :], nets)
        victim_ref[k] = mm(hot, nets_ref[...]).astype(bf16)
    victim_ref.flush()
    for asked_ref, near_ref in zip(asked_refs, near_refs, strict=True):
        hot = onehot_rows(asked_ref[...], nets)
        near_ref[...] = mm(hot, nets_ref[...]).astype(bf16)
    for k in range(regions):
        linear_ref[k] = mm(victim_ref[k], w1_ref[:feat, :])


def pair_kernel(rid_ref, count_ref, target_ref, linear_ref, w1_ref, w2_ref, *refs, ks, first, last):
    some = len(ks)
    slots, hid = linear_ref.shape[1:]
    feat = refs[0].shape[1]
    me = rid_ref[0]
    partner_refs, refs = refs[:some], refs[some:]
    if last:
        victim_ref, refs = refs[0], refs[1:]
        others = victim_ref.shape[0] - some
        old_partner_refs, old_lin_ref, refs = refs[:others], refs[others], refs[others + 1 :]
    if not first:
        before_ref, refs = refs[0], refs[1:]
    lin_grad_ref, sums_ref, *back_refs = refs
    across = []
    w2_row = w2_ref[...].astype(f32)
    w2_column = column_of(w2_row).astype(bf16)
    w2_sum = jnp.zeros((1, hid), f32) if first else before_ref[0:1, :]
    sq_sum = jnp.zeros((1, hid), f32) if first else before_ref[1:2, :]
    slot = lax.broadcasted_iota(i32, (slots, 128), 0)
    for at, k in enumerate(ks):
        linear = linear_ref[k] + mm(partner_refs[at][...], w1_ref[feat:, :])
        square = linear * linear
        inner = gelu_inner(linear, square)
        half = 0.5 * linear
        activated = (half + half * inner).astype(bf16)
        scores = mm(activated, w2_column)
        live = slot < count_ref[0, me ^ k]
        errors = jnp.where(live, scores - column_of(target_ref[pl.ds(me ^ k, 1), :]), 0.0)
        errors = jnp.concatenate([errors] * (hid // 128), 1)
        sq_sum = sq_sum + jnp.sum(errors * errors, 0, keepdims=True)
        residual = 2.0 * errors
        w2_sum = w2_sum + jnp.sum(residual * activated.astype(f32), 0, keepdims=True)
        lin_grad = (residual * w2_row * slope_of(linear, square, inner)).astype(bf16)
        lin_grad_ref[at] = lin_grad
        lin_grad_ref.flush(at + 1)
        back = mm_dims(lin_grad, w1_ref[feat:, :], NT).astype(bf16)
        pieces = len(back_refs) // some
        rows = slots // pieces
        for piece in range(pieces):
            back_refs[at * pieces + piece][...] = back[piece * rows : (piece + 1) * rows]
        if last:
            across.append(lin_grad.T)
    if not last:
        sums_ref[...] = jnp.concatenate([w2_sum, sq_sum, jnp.zeros((6, hid), f32)], 0)
        return
    for at in range(others):
        across.append(old_lin_ref[at].T)
    across = jnp.concatenate(across, 1)
    victims = jnp.concatenate([victim_ref[k] for k in range(some + others)], 0)
    partners = jnp.concatenate([ref[...] for ref in [*partner_refs, *old_partner_refs]], 0)
    both = jnp.concatenate([mm(across, victims).T, mm(across, partners).T], 0)
    count = count_ref[0, 0]
    for q in range(1, count_ref.shape[1]):
        count = count + count_ref[0, q]
    count_row = jnp.zeros((1, hid), f32) + count.astype(f32)
    parts = []
    for row in (w2_sum, sq_sum, count_row):
        high = row.astype(bf16).astype(f32)
        parts += [high, row - high]
    short = jnp.concatenate(parts + [jnp.zeros((2, hid), f32)], 0)
    devices = sums_ref.shape[0]
    share = 2 * feat // devices
    for d in range(devices):
        sums_ref[d] = jnp.concatenate([both[d * share : (d + 1) * share], short], 0).astype(bf16)


def local_grad_kernel(rid_ref, local_ref, w1_ref, after_ref, *refs, groups, near):
    regions, slots = local_ref.shape
    asked_refs, refs = refs[:near], refs[near:]
    near_refs, refs = refs[: 2 * near], refs[2 * near :]
    lin_refs, (grad_ref, vg_ref) = refs[: len(groups)], refs[len(groups) :]
    nets, feat = grad_ref.shape
    me = rid_ref[0]
    returned = jnp.concatenate([near_ref[...] for near_ref in near_refs], 0)
    for at in range(0, nets, BLOCK):
        hot = jnp.concatenate([onehot_cols(ref[...], at, BLOCK) for ref in asked_refs], 1)
        grad_ref[at : at + BLOCK, :] = mm(hot, returned)
    for ref, ks in zip(lin_refs, groups, strict=True):
        for at, k in enumerate(ks):
            vg_ref[k * slots : (k + 1) * slots, :] = mm_dims(ref[at], w1_ref[:feat, :], NT).astype(
                bf16
            )
    listed = [local_ref[pl.ds(me ^ k, 1), :] for k in range(regions)]
    for at in range(0, nets, BLOCK):
        hot = jnp.concatenate([onehot_cols(row, at, BLOCK) for row in listed], 1)
        grad_ref[at : at + BLOCK, :] += mm(hot, vg_ref[...])
        if (at + BLOCK) * PARTS % nets == 0:
            grad_ref.flush(at + BLOCK)


def layer_grad_kernel(
    cid_ref, grad_ref, slope_ref, gnn_ref, embeds_ref, agg_ref, halo_ref, *refs, far, order, degree
):
    asked_refs, refs = refs[:far], refs[far:]
    far_refs, refs = refs[:far], refs[far:]
    (rest_ref, agg_grad_ref, gnn_out_ref), refs = refs[:3], refs[3:]
    back_refs, (back_ref, total_ref) = refs[:-2], refs[-2:]
    nets, feat = grad_ref.shape
    halo = back_refs[0].shape[0]
    top = jnp.zeros((feat, feat), f32)
    low = jnp.zeros((feat, feat), f32)
    returned = jnp.concatenate([ref[...] for ref in far_refs], 0)
    for at in range(0, nets, STEP):
        hot = jnp.concatenate([onehot_cols(ref[...], at, STEP) for ref in asked_refs], 1)
        total_ref[pl.ds(at, STEP), :] = mm(hot, returned)
    for at in range(0, nets, STEP):
        rows = pl.ds(at, STEP)
        total = total_ref[rows, :] + grad_ref[rows, :]
        pre_grad = (total * slope_ref[rows, :].astype(f32)).astype(bf16)
        agg_grad = mm_dims(pre_grad, gnn_ref[feat:, :], NT)
        agg_grad = (agg_grad * (1.0 / degree)).astype(bf16)
        agg_grad_ref[rows, :] = agg_grad
        rest_ref[rows, :] = (total + mm_dims(pre_grad, gnn_ref[:feat, :], NT)).astype(bf16)
        if (at + STEP) * 2 % nets == 0:
            rest_ref.flush(at + STEP)
            agg_grad_ref.flush(at + STEP)
        top = top + mm_dims(embeds_ref[rows, :], pre_grad, TT)
        low = low + mm_dims(agg_ref[rows, :], pre_grad, TT)
    gnn_out_ref[:feat, :] = top.astype(bf16)
    gnn_out_ref[feat:, :] = low.astype(bf16)
    gnn_out_ref.flush()
    back = jnp.zeros(back_ref.shape, f32)
    for at in range(0, nets, STEP):
        back = back + mm(halo_ref[at // STEP], agg_grad_ref[pl.ds(at, STEP), :])
    back_ref[...] = back.astype(bf16)
    me = cid_ref[0]
    for k, out_ref in zip(order, back_refs, strict=True):
        out_ref[...] = back_ref[pl.ds(pl.multiple_of((me ^ k) * halo, halo), halo), :]


def share_kernel(w1_ref, gnn_ref, wide_ref, short_ref, *, nets_total, doms):
    share, hid = gnn_ref.shape[1:]
    w1_sum = jnp.sum(w1_ref[...].astype(f32), 0)
    gnn_sum = jnp.sum(gnn_ref[...].astype(f32), 0)
    short = w1_sum[share:]
    w2_sum = short[0:1] + short[1:2]
    sq_sum = short[2:3] + short[3:4]
    count = short[4:5] + short[5:6]
    factor = 8.0 / jnp.sqrt(count)
    halves = [(w1_sum[:share] * factor).astype(bf16), (gnn_sum * factor).astype(bf16)]
    for d in range(wide_ref.shape[0]):
        wide_ref[d] = halves[d // doms % 2]
    short_ref[...] = jnp.concatenate(
        [w2_sum * factor, sq_sum / count, 8.0 * nets_total / count, jnp.zeros((5, hid), f32)], 0
    )


def unpack_kernel(rid_ref, mine_ref, other_ref, w1_ref, gnn_ref):
    devices, share, _ = mine_ref.shape
    even = rid_ref[0] % 2 == 0
    for d in range(devices):
        rows = slice(d * share, (d + 1) * share)
        mine, other = mine_ref[d].astype(f32), other_ref[d].astype(f32)
        w1_ref[rows, :] = jnp.where(even, mine, other)
        gnn_ref[rows, :] = jnp.where(even, other, mine)
        if (d + 1) % (devices // PARTS) == 0:
            w1_ref.flush((d + 1) * share)
            gnn_ref.flush((d + 1) * share)


def final_kernel(cid_ref, short_ref, send_ref, agg_grad_ref, own_ref, rest_ref, *refs):
    got_refs, (out_ref, w2_ref, loss_ref, sum_ref) = refs[:-4], refs[-4:]
    w2_ref[...] = short_ref[0:1, :]
    loss_ref[...] = short_ref[1:2, :]
    nets = out_ref.shape[0]
    me = cid_ref[0]
    scale = short_ref[2:3, :]
    got = jnp.concatenate([ref[...] for ref in got_refs], 0)
    sent = [send_ref[pl.ds(me ^ k, 1), :] for k in range(len(got_refs))]
    for at in range(0, nets, BLOCK):
        hot = jnp.concatenate([onehot_cols(row, at, BLOCK) for row in sent], 1)
        sum_ref[at : at + BLOCK, :] = mm(hot, got)
    steps = own_ref.shape[0]
    for half in range(2):
        mine = range(half * steps // 2, (half + 1) * steps // 2)
        given = agg_grad_ref[pl.ds(half * nets // 2, nets // 2), :]
        for at in range(0, nets, BLOCK):
            rows = pl.ds(at, BLOCK)
            parts = jnp.concatenate([own_ref[i, rows, :] for i in mine], 1)
            total = sum_ref[rows, :] + mm(parts, given)
            if half == 0:
                sum_ref[rows, :] = total
                continue
            out_ref[rows, :] = ((total + rest_ref[rows, :]) * scale).astype(bf16)
            if (at + BLOCK) * PARTS % nets == 0:
                out_ref.flush(at + BLOCK)


SM = pl.BlockSpec(memory_space=pltpu.SMEM)
VM = pl.BlockSpec(memory_space=pltpu.VMEM)
ANY = pl.BlockSpec(memory_space=pl.ANY)
SMALL = pl.CostEstimate(flops=1, bytes_accessed=1, transcendentals=0)
PARTS = 4


def shape(dims, dtype):
    return jax.ShapeDtypeStruct(dims, dtype)


def in_hbm(dims, dtype):
    return pltpu.MemorySpace.HBM(dims, dtype)


class Load:
    def __init__(self, source, target, sems, parts):
        self.target, self.shape, self.waited = target, source.shape, 0
        self.rows = source.shape[0] // parts
        self.copies = []
        for at in range(parts):
            part = pl.ds(at * self.rows, self.rows)
            self.copies.append(
                pltpu.make_async_copy(source.at[part], target.at[part], sems.at[at])
            )
            self.copies[-1].start()

    def wait(self, upto=None):
        upto = self.shape[0] if upto is None else upto
        while self.waited * self.rows < upto:
            self.copies[self.waited].wait()
            self.waited += 1

    def __getitem__(self, index):
        first = index[0] if isinstance(index, tuple) else index
        self.wait(first + 1 if isinstance(first, int) else None)
        return self.target[index]


class Store:
    def __init__(self, source, target, sems):
        self.source, self.target, self.sems = source, target, sems
        self.shape, self.dtype = source.shape, source.dtype
        self.copies, self.sent = [], 0

    def __setitem__(self, index, value):
        self.source[index] = value

    def __getitem__(self, index):
        return self.source[index]

    def flush(self, upto=None):
        upto = self.shape[0] if upto is None else upto
        part = pl.ds(self.sent, upto - self.sent)
        self.copies.append(
            pltpu.make_async_copy(
                self.source.at[part], self.target.at[part], self.sems.at[len(self.copies)]
            )
        )
        self.copies[-1].start()
        self.sent = upto

    def finish(self):
        if self.sent < self.shape[0]:
            self.flush()
        for copy in self.copies:
            copy.wait()


def call(kernel, name, outs, args, scratch=(), mib=32, flops=1, halves=-1):
    ins = [kind for _, kind in args]
    kinds = [kind for _, _, kind in outs]
    staged = [pltpu.VMEM(value.shape, value.dtype) for value, kind in args if kind == "H"]
    staged += [pltpu.VMEM(dims, dtype) for dims, dtype, kind in outs if kind == "H"]
    moved = len(staged)

    def body(*refs):
        operands, refs = list(refs[: len(ins)]), refs[len(ins) :]
        results, refs = list(refs[: len(kinds)]), refs[len(kinds) :]
        buffers, refs = list(refs[:moved]), refs[moved:]
        if moved:
            sems, refs = refs[0], refs[1:]
        at = 0
        for i, kind in enumerate(ins):
            if kind == "H":
                parts = 2 if i == halves else 1
                operands[i] = Load(operands[i], buffers[at], sems.at[at], parts)
                at += 1
        for i, kind in enumerate(kinds):
            if kind == "H":
                results[i] = Store(buffers[at], results[i], sems.at[at])
                at += 1
        kernel(*operands, *results, *refs)
        for operand in operands:
            if isinstance(operand, Load):
                operand.wait()
        for result in results:
            if isinstance(result, Store):
                result.finish()

    spec_of = {"V": VM, "H": ANY, "S": SM, "A": ANY}
    return pl.pallas_call(
        body,
        out_shape=[(in_hbm if kind == "H" else shape)(dims, dtype) for dims, dtype, kind in outs],
        in_specs=[spec_of[kind] for kind in ins],
        out_specs=[spec_of[kind] for kind in kinds],
        scratch_shapes=staged
        + ([pltpu.SemaphoreType.DMA((moved, 2 * PARTS))] if moved else [])
        + list(scratch),
        compiler_params=pltpu.CompilerParams(vmem_limit_bytes=mib << 20),
        cost_estimate=pl.CostEstimate(flops=flops, bytes_accessed=1, transcendentals=0),
        name=name,
    )(
        *[
            pltpu.with_memory_space_constraint(value, pltpu.HBM) if kind == "H" else value
            for value, kind in args
        ]
    )


def exchange(value, axis):
    return lax.all_to_all(value, axis, split_axis=0, concat_axis=0, tiled=True)


def local(
    embeds,
    neighbours,
    halo_send,
    gnn_weight,
    pair_local,
    pair_remote,
    pair_count,
    targets,
    pair_w1,
    pair_w2,
):
    nets, feat = embeds.shape
    hid = pair_w1.shape[1]
    degree = neighbours.shape[1]
    regions, slots = pair_local.shape
    peers, halo = halo_send.shape
    halo_rows = peers * halo
    devices = lax.axis_size("region") * lax.axis_size("dom")
    my_region = lax.axis_index("region").astype(i32)
    rid = my_region.reshape(1)
    cid = lax.axis_index("dom").astype(i32).reshape(1)
    near = 2
    far = regions - near
    share = 2 * feat // devices

    def permute(value, k, axis="region"):
        size = lax.axis_size(axis)
        return lax.ppermute(value, axis, [(i, i ^ k) for i in range(size)])

    def v(*values):
        return [(value, "V") for value in values]

    def h(*values):
        return [(value, "H") for value in values]

    def out(kind, dtype, *dims):
        return [(dims, dtype, kind)]

    (outgoing,) = call(
        halo_gather_kernel,
        "halo_gather",
        out("V", bf16, halo_rows, feat),
        h(halo_send, embeds),
    )
    received = exchange(outgoing.reshape(peers, halo, feat), "dom").reshape(halo_rows, feat)

    wanted = [lax.dynamic_slice_in_dim(pair_remote, my_region ^ k, 1, 0) for k in range(regions)]
    asked = [wanted[0]] + [permute(wanted[k], k) for k in range(1, regions)]

    steps = nets // STEP
    own, from_halo, agg_sum = pl.pallas_call(
        adjacency_kernel,
        grid=(steps,),
        in_specs=[
            pl.BlockSpec((degree, STEP), lambda i: (0, i)),
            pl.BlockSpec((nets, feat), lambda i: (0, 0)),
        ],
        out_specs=[
            pl.BlockSpec((1, nets, STEP), lambda i: (i, 0, 0)),
            pl.BlockSpec((1, halo_rows, STEP), lambda i: (i, 0, 0)),
            pl.BlockSpec((STEP, feat), lambda i: (i, 0)),
        ],
        out_shape=[
            in_hbm((steps, nets, STEP), bf16),
            in_hbm((steps, halo_rows, STEP), bf16),
            in_hbm((nets, feat), f32),
        ],
        scratch_shapes=[pltpu.VMEM((feat, nets), bf16)],
        compiler_params=pltpu.CompilerParams(vmem_limit_bytes=24 << 20),
        cost_estimate=SMALL,
        name="adjacency",
    )(neighbours.T, embeds)

    pre, aggregate, net_values, *far_sends = call(
        functools.partial(layer_kernel, degree=degree, far=far),
        "layer",
        out("V", f32, nets, feat)
        + out("H", bf16, nets, feat)
        + out("V", bf16, nets, feat)
        + out("V", bf16, slots, feat) * far,
        h(from_halo, agg_sum) + v(embeds, gnn_weight, received, *asked[near:]),
        [pltpu.VMEM((far, slots, nets), bf16)],
    )
    victim, linear_own, slope, *near_sends = call(
        functools.partial(victim_kernel, near=near),
        "victims",
        out("H", bf16, regions, slots, feat)
        + out("V", f32, regions, slots, hid)
        + out("H", bf16, nets, feat)
        + out("V", bf16, slots, feat) * near,
        [(rid, "S")] + v(pair_local, net_values) + h(pair_w1) + v(pre, *asked[:near]),
        flops=VICTIMS,
    )
    partners = [near_sends[0]]
    partners += [permute(near_sends[k], k) for k in range(1, near)]
    partners += [permute(far_sends[k - near], k) for k in range(near, regions)]

    groups = [tuple(range(near, regions)), tuple(range(near))]
    w2_row = pair_w2.reshape(1, hid)
    lin_grads, backs, sums = [], {}, []
    for ks in groups:
        last = ks is groups[-1]
        pieces = 2 if last else 1
        lin_grad, sums_now, *back = call(
            functools.partial(pair_kernel, ks=ks, first=ks is groups[0], last=last),
            "pairs",
            out("H", bf16, len(ks), slots, hid)
            + (out("V", bf16, devices, share + 8, hid) if last else out("V", f32, 8, hid))
            + out("V", bf16, slots // pieces, feat) * (pieces * len(ks)),
            [(rid, "S"), (pair_count, "S")]
            + v(targets, linear_own, pair_w1, w2_row)
            + v(*[partners[k] for k in ks])
            + (h(victim, *partners[near:], *lin_grads) if last else [])
            + v(*sums),
            flops=PAIRS,
        )
        lin_grads.append(lin_grad)
        for at, k in enumerate(ks):
            backs[k] = back[at * pieces : (at + 1) * pieces]
        sums = [sums_now]
    returned = [backs[0]] + [[permute(x, k) for x in backs[k]] for k in range(1, regions)]

    (w1_parts,) = sums
    w1_got = exchange(w1_parts, BOTH)
    (local_grad,) = call(
        functools.partial(local_grad_kernel, groups=groups, near=near),
        "local_grads",
        out("H", f32, nets, feat),
        [(rid, "S")]
        + v(pair_local)
        + h(pair_w1)
        + [(w1_parts, "A")]
        + v(*asked[:near], *sum(returned[:near], []))
        + h(*lin_grads),
        [pltpu.VMEM((regions * slots, feat), bf16)],
        flops=LOCAL,
    )
    order = [0, 1, *range(peers - 1, 1, -1)]
    rest, agg_grad, gnn_part, *backs = call(
        functools.partial(layer_grad_kernel, far=far, order=order, degree=degree),
        "layer_grad",
        out("H", bf16, nets, feat) * 2
        + out("H", bf16, 2 * feat, feat)
        + out("V", bf16, halo, feat) * peers,
        [(cid, "S")]
        + h(local_grad, slope)
        + v(gnn_weight, embeds)
        + h(aggregate, from_halo)
        + v(*asked[near:], *sum(returned[near:], [])),
        [pltpu.VMEM((halo_rows, feat), bf16), pltpu.VMEM((nets, feat), f32)],
        flops=10**10,
    )
    gnn_part, w1_got = lax.optimization_barrier((gnn_part, w1_got))
    gnn_got = exchange(gnn_part.reshape(devices, share, feat), BOTH)
    backs = dict(zip(order, backs, strict=True))
    returned_halo = [backs[0]] + [permute(backs[k], k, "dom") for k in range(1, peers)]

    wide, short = call(
        functools.partial(share_kernel, nets_total=nets * devices, doms=peers),
        "shares",
        out("V", bf16, devices, share, feat) + out("V", f32, 8, hid),
        v(w1_got, gnn_got),
        flops=SHARES,
    )
    spread = exchange(wide, BOTH)

    embeds_grad, w2_grad, loss = call(
        final_kernel,
        "embeds_grads",
        out("H", bf16, nets, feat) + out("V", f32, 1, hid) * 2,
        [(cid, "S")] + v(short, halo_send) + h(agg_grad, own, rest) + v(*returned_halo),
        [pltpu.VMEM((nets, feat), f32)],
        flops=FINAL,
        halves=4,
    )
    spread, w2_grad = lax.optimization_barrier((spread, w2_grad))
    w1_grad, gnn_grad = call(
        unpack_kernel,
        "unpack",
        out("H", f32, 2 * feat, hid) + out("H", f32, 2 * feat, feat),
        [(rid, "S")] + v(spread, permute(spread, 1)),
    )
    return embeds_grad, gnn_grad, w1_grad, w2_grad[0], loss[0, 0]


def solution(mesh):
    split = P(BOTH, None)
    in_specs = (split, split, split, P(), split, split, split, split, P(), P())
    out_specs = (split, P(), P(), P(), P())
    return jax.shard_map(local, mesh=mesh, in_specs=in_specs, out_specs=out_specs, check_vma=False)
```

```python
import functools
import math

import jax
import jax.numpy as jnp
from jax import lax
from jax.experimental import pallas as pl
from jax.experimental.pallas import tpu as pltpu
from jax.sharding import PartitionSpec as P

bf16 = jnp.bfloat16
f32 = jnp.float32
i32 = jnp.int32
i16 = jnp.int16
gelu_coef = 0.7978845608
BOTH = ("region", "dom")
BLOCK = 256
VICTIMS = 10**10
PAIRS = 2 * 10**9
LOCAL = 1
SHARES = 1
FINAL = 2 * 10**10
STEP = 512
TT = (((0,), (0,)), ((), ()))
NT = (((1,), (1,)), ((), ()))


def mm(a, b):
    return jnp.dot(a, b, preferred_element_type=f32)


def mm_dims(a, b, dims):
    return lax.dot_general(a, b, dims, preferred_element_type=f32)


def gelu_inner(value, square):
    return jnp.tanh(value * (gelu_coef + (gelu_coef * 0.044715) * square))


def gelu_of(value):
    half = 0.5 * value
    return half + half * gelu_inner(value, value * value)


def slope_of(value, square, inner):
    rise = value * (0.5 * gelu_coef + (1.5 * 0.044715 * gelu_coef) * square)
    return 0.5 + 0.5 * inner + (1.0 - inner * inner) * rise


def column_of(row):
    return jnp.broadcast_to(row, (128, row.shape[1])).T


def onehot_rows(row, width):
    column = column_of(row).astype(i16)
    lane = lax.broadcasted_iota(i32, (16, 128), 1)
    one = jnp.ones(column.shape, bf16)
    zero = jnp.zeros(column.shape, bf16)
    tiles = []
    for j in range(width // 128):
        lanes = jnp.concatenate([(lane + 128 * j).astype(i16)] * (column.shape[0] // 16), 0)
        tiles.append(jnp.where(column == lanes, one, zero))
    return jnp.concatenate(tiles, 1)


def onehot_cols(row, first, height):
    width = row.shape[1]
    wide = jnp.broadcast_to(row, (16, width)).astype(i16)
    wide = jnp.concatenate([wide] * (height // 16), 0)
    sub = (lax.broadcasted_iota(i32, (height, 128), 0) + first).astype(i16)
    sub = jnp.concatenate([sub] * (width // 128), 1)
    return jnp.where(wide == sub, jnp.ones(wide.shape, bf16), jnp.zeros(wide.shape, bf16))


def halo_gather_kernel(send_ref, embeds_ref, out_ref):
    peers, halo = send_ref.shape
    nets = embeds_ref.shape[0]
    group = max(peers // 2, 1)
    sent = send_ref[...]
    hots = [
        jnp.concatenate([onehot_rows(sent[q : q + 1, :], nets) for q in range(p, p + group)], 0)
        for p in range(0, peers, group)
    ]
    for at, hot in enumerate(hots):
        rows = slice(at * group * halo, (at + 1) * group * halo)
        out_ref[rows, :] = mm(hot, embeds_ref[...]).astype(bf16)


def adjacency_kernel(neigh_ref, embeds_ref, own_ref, halo_ref, sum_ref, across_ref):
    degree, rows = neigh_ref.shape
    nets, halo_rows = own_ref.shape[1], halo_ref.shape[1]

    @pl.when(pl.program_id(0) == 0)
    def turn():
        across_ref[...] = embeds_ref[...].T

    listed = neigh_ref[...]
    low = listed & 127
    high = listed >> 7
    bit = jnp.left_shift(jnp.ones_like(listed), (high & 7) * 4)
    words = -(-(nets + halo_rows) // 1024)
    parts = [jnp.where((high >> 3) == k, bit, 0) for k in range(words)]
    for first in range(0, 128, 32):
        sub = lax.broadcasted_iota(i32, (32, rows), 0) + first
        packed = [jnp.zeros((32, rows), i32) for _ in range(words)]
        for c in range(degree):
            same = sub == low[c : c + 1, :]
            for k in range(words):
                packed[k] = packed[k] + jnp.where(same, parts[k][c : c + 1, :], 0)
        for at in range(0, nets + halo_rows, 128):
            j = at // 128
            counts = ((packed[j // 8] >> (4 * (j % 8))) & 15).astype(f32).astype(bf16)
            if at < nets:
                own_ref[0, at + first : at + first + 32, :] = counts
            else:
                halo_ref[0, at - nets + first : at - nets + first + 32, :] = counts
    sum_ref[...] = mm(across_ref[...], own_ref[0]).T


def layer_kernel(halo_ref, sum_ref, embeds_ref, gnn_ref, received_ref, *refs, degree, far):
    asked_refs, (pre_ref, agg_ref, nets_ref), send_refs = (
        refs[:far],
        refs[far : far + 3],
        refs[far + 3 : -1],
    )
    hot_ref = refs[-1]
    nets, feat = nets_ref.shape
    across = received_ref[...].T
    for k, asked_ref in enumerate(asked_refs):
        hot_ref[k] = onehot_rows(asked_ref[...], nets)
    for at in range(0, nets, STEP):
        rows = pl.ds(at, STEP)
        pre_ref[rows, :] = mm(embeds_ref[rows, :], gnn_ref[:feat, :])
    for at in range(0, nets, STEP):
        rows = pl.ds(at, STEP)
        total = mm(across, halo_ref[at // STEP]).T
        total = total + sum_ref[rows, :]
        agg = (total * (1.0 / degree)).astype(bf16)
        agg_ref[rows, :] = agg
        agg_ref.flush(at + STEP)
        pre = pre_ref[rows, :] + mm(agg, gnn_ref[feat:, :])
        pre_ref[rows, :] = pre
        nets_ref[rows, :] = (embeds_ref[rows, :].astype(f32) + gelu_of(pre)).astype(bf16)
    for k, send_ref in enumerate(send_refs):
        send_ref[...] = mm(hot_ref[k], nets_ref[...]).astype(bf16)


def victim_kernel(
    rid_ref, local_ref, nets_ref, w1_ref, pre_ref, *refs, near
):
    asked_refs, (victim_ref, linear_ref, slope_ref), near_refs = (
        refs[:near],
        refs[near : near + 3],
        refs[near + 3 :],
    )
    regions, slots = local_ref.shape
    nets, feat = nets_ref.shape
    me = rid_ref[0]
    for at in range(0, nets, STEP):
        rows = pl.ds(at, STEP)
        pre = pre_ref[rows, :]
        square = pre * pre
        slope_ref[rows, :] = slope_of(pre, square, gelu_inner(pre, square)).astype(bf16)
    slope_ref.flush()
    for k in range(regions):
        hot = onehot_rows(local_ref[pl.ds(me ^ k, 1), :], nets)
        victim_ref[k] = mm(hot, nets_ref[...]).astype(bf16)
    victim_ref.flush()
    for asked_ref, near_ref in zip(asked_refs, near_refs, strict=True):
        hot = onehot_rows(asked_ref[...], nets)
        near_ref[...] = mm(hot, nets_ref[...]).astype(bf16)
    for k in range(regions):
        linear_ref[k] = mm(victim_ref[k], w1_ref[:feat, :])


def pair_kernel(rid_ref, count_ref, target_ref, linear_ref, w1_ref, w2_ref, *refs, ks, first, last):
    some = len(ks)
    slots, hid = linear_ref.shape[1:]
    feat = refs[0].shape[1]
    me = rid_ref[0]
    partner_refs, refs = refs[:some], refs[some:]
    if last:
        victim_ref, refs = refs[0], refs[1:]
        others = victim_ref.shape[0] - some
        old_partner_refs, old_lin_ref, refs = refs[:others], refs[others], refs[others + 1 :]
    if not first:
        before_ref, refs = refs[0], refs[1:]
    lin_grad_ref, sums_ref, *back_refs = refs
    across = []
    w2_row = w2_ref[...].astype(f32)
    w2_column = column_of(w2_row).astype(bf16)
    w2_sum = jnp.zeros((1, hid), f32) if first else before_ref[0:1, :]
    sq_sum = jnp.zeros((1, hid), f32) if first else before_ref[1:2, :]
    slot = lax.broadcasted_iota(i32, (slots, 128), 0)
    for at, k in enumerate(ks):
        linear = linear_ref[k] + mm(partner_refs[at][...], w1_ref[feat:, :])
        square = linear * linear
        inner = gelu_inner(linear, square)
        half = 0.5 * linear
        activated = (half + half * inner).astype(bf16)
        scores = mm(activated, w2_column)
        live = slot < count_ref[0, me ^ k]
        errors = jnp.where(live, scores - column_of(target_ref[pl.ds(me ^ k, 1), :]), 0.0)
        errors = jnp.concatenate([errors] * (hid // 128), 1)
        sq_sum = sq_sum + jnp.sum(errors * errors, 0, keepdims=True)
        residual = 2.0 * errors
        w2_sum = w2_sum + jnp.sum(residual * activated.astype(f32), 0, keepdims=True)
        lin_grad = (residual * w2_row * slope_of(linear, square, inner)).astype(bf16)
        lin_grad_ref[at] = lin_grad
        lin_grad_ref.flush(at + 1)
        back = mm_dims(lin_grad, w1_ref[feat:, :], NT).astype(bf16)
        pieces = len(back_refs) // some
        rows = slots // pieces
        for piece in range(pieces):
            back_refs[at * pieces + piece][...] = back[piece * rows : (piece + 1) * rows]
        if last:
            across.append(lin_grad.T)
    if not last:
        sums_ref[...] = jnp.concatenate([w2_sum, sq_sum, jnp.zeros((6, hid), f32)], 0)
        return
    for at in range(others):
        across.append(old_lin_ref[at].T)
    across = jnp.concatenate(across, 1)
    victims = jnp.concatenate([victim_ref[k] for k in range(some + others)], 0)
    partners = jnp.concatenate([ref[...] for ref in [*partner_refs, *old_partner_refs]], 0)
    both = jnp.concatenate([mm(across, victims).T, mm(across, partners).T], 0)
    count = count_ref[0, 0]
    for q in range(1, count_ref.shape[1]):
        count = count + count_ref[0, q]
    count_row = jnp.zeros((1, hid), f32) + count.astype(f32)
    parts = []
    for row in (w2_sum, sq_sum, count_row):
        high = row.astype(bf16).astype(f32)
        parts += [high, row - high]
    short = jnp.concatenate(parts + [jnp.zeros((2, hid), f32)], 0)
    devices = sums_ref.shape[0]
    share = 2 * feat // devices
    for d in range(devices):
        sums_ref[d] = jnp.concatenate([both[d * share : (d + 1) * share], short], 0).astype(bf16)


def local_grad_kernel(rid_ref, local_ref, w1_ref, after_ref, *refs, groups, near):
    regions, slots = local_ref.shape
    asked_refs, refs = refs[:near], refs[near:]
    near_refs, refs = refs[: 2 * near], refs[2 * near :]
    lin_refs, (grad_ref, vg_ref, sum_ref) = refs[: len(groups)], refs[len(groups) :]
    nets, feat = grad_ref.shape
    me = rid_ref[0]
    returned = jnp.concatenate([near_ref[...] for near_ref in near_refs], 0)
    for at in range(0, nets, BLOCK):
        hot = jnp.concatenate([onehot_cols(ref[...], at, BLOCK) for ref in asked_refs], 1)
        sum_ref[at : at + BLOCK, :] = mm(hot, returned)
    for ref, ks in zip(lin_refs, groups, strict=True):
        for at, k in enumerate(ks):
            vg_ref[k * slots : (k + 1) * slots, :] = mm_dims(ref[at], w1_ref[:feat, :], NT).astype(
                bf16
            )
    listed = [local_ref[pl.ds(me ^ k, 1), :] for k in range(regions)]
    for at in range(0, nets, BLOCK):
        hot = jnp.concatenate([onehot_cols(row, at, BLOCK) for row in listed], 1)
        total = sum_ref[at : at + BLOCK, :] + mm(hot, vg_ref[...])
        grad_ref[at : at + BLOCK, :] = total.astype(bf16)
        if (at + BLOCK) * PARTS % nets == 0:
            grad_ref.flush(at + BLOCK)


def layer_grad_kernel(
    cid_ref, grad_ref, slope_ref, gnn_ref, embeds_ref, agg_ref, halo_ref, *refs, far, order, degree
):
    asked_refs, refs = refs[:far], refs[far:]
    far_refs, refs = refs[:far], refs[far:]
    (rest_ref, agg_grad_ref, gnn_out_ref), refs = refs[:3], refs[3:]
    back_refs, (back_ref, total_ref) = refs[:-2], refs[-2:]
    nets, feat = grad_ref.shape
    halo = back_refs[0].shape[0]
    top = jnp.zeros((feat, feat), f32)
    low = jnp.zeros((feat, feat), f32)
    returned = jnp.concatenate([ref[...] for ref in far_refs], 0)
    for at in range(0, nets, STEP):
        hot = jnp.concatenate([onehot_cols(ref[...], at, STEP) for ref in asked_refs], 1)
        total_ref[pl.ds(at, STEP), :] = mm(hot, returned)
    for at in range(0, nets, STEP):
        rows = pl.ds(at, STEP)
        total = total_ref[rows, :] + grad_ref[rows, :].astype(f32)
        pre_grad = (total * slope_ref[rows, :].astype(f32)).astype(bf16)
        agg_grad = mm_dims(pre_grad, gnn_ref[feat:, :], NT)
        agg_grad = (agg_grad * (1.0 / degree)).astype(bf16)
        agg_grad_ref[rows, :] = agg_grad
        rest_ref[rows, :] = (total + mm_dims(pre_grad, gnn_ref[:feat, :], NT)).astype(bf16)
        if (at + STEP) * 2 % nets == 0:
            rest_ref.flush(at + STEP)
            agg_grad_ref.flush(at + STEP)
        top = top + mm_dims(embeds_ref[rows, :], pre_grad, TT)
        low = low + mm_dims(agg_ref[rows, :], pre_grad, TT)
    gnn_out_ref[:feat, :] = top.astype(bf16)
    gnn_out_ref[feat:, :] = low.astype(bf16)
    gnn_out_ref.flush()
    back = jnp.zeros(back_ref.shape, f32)
    for at in range(0, nets, STEP):
        back = back + mm(halo_ref[at // STEP], agg_grad_ref[pl.ds(at, STEP), :])
    back_ref[...] = back.astype(bf16)
    me = cid_ref[0]
    for k, out_ref in zip(order, back_refs, strict=True):
        out_ref[...] = back_ref[pl.ds(pl.multiple_of((me ^ k) * halo, halo), halo), :]


def share_kernel(w1_ref, gnn_ref, wide_ref, short_ref, *, nets_total, doms):
    share, hid = gnn_ref.shape[1:]
    w1_sum = jnp.sum(w1_ref[...].astype(f32), 0)
    gnn_sum = jnp.sum(gnn_ref[...].astype(f32), 0)
    short = w1_sum[share:]
    w2_sum = short[0:1] + short[1:2]
    sq_sum = short[2:3] + short[3:4]
    count = short[4:5] + short[5:6]
    factor = 8.0 / jnp.sqrt(count)
    halves = [(w1_sum[:share] * factor).astype(bf16), (gnn_sum * factor).astype(bf16)]
    for d in range(wide_ref.shape[0]):
        wide_ref[d] = halves[d // doms % 2]
    short_ref[...] = jnp.concatenate(
        [w2_sum * factor, sq_sum / count, 8.0 * nets_total / count, jnp.zeros((5, hid), f32)], 0
    )


def unpack_kernel(rid_ref, mine_ref, other_ref, w1_ref, gnn_ref):
    devices, share, _ = mine_ref.shape
    even = rid_ref[0] % 2 == 0
    for d in range(devices):
        rows = slice(d * share, (d + 1) * share)
        mine, other = mine_ref[d].astype(f32), other_ref[d].astype(f32)
        w1_ref[rows, :] = jnp.where(even, mine, other)
        gnn_ref[rows, :] = jnp.where(even, other, mine)
        if (d + 1) % (devices // PARTS) == 0:
            w1_ref.flush((d + 1) * share)
            gnn_ref.flush((d + 1) * share)


def final_kernel(cid_ref, short_ref, send_ref, agg_grad_ref, own_ref, rest_ref, *refs):
    got_refs, (out_ref, w2_ref, loss_ref, sum_ref) = refs[:-4], refs[-4:]
    w2_ref[...] = short_ref[0:1, :]
    loss_ref[...] = short_ref[1:2, :]
    nets = out_ref.shape[0]
    me = cid_ref[0]
    scale = short_ref[2:3, :]
    got = jnp.concatenate([ref[...] for ref in got_refs], 0)
    sent = [send_ref[pl.ds(me ^ k, 1), :] for k in range(len(got_refs))]
    for at in range(0, nets, BLOCK):
        hot = jnp.concatenate([onehot_cols(row, at, BLOCK) for row in sent], 1)
        sum_ref[at : at + BLOCK, :] = mm(hot, got)
    steps = own_ref.shape[0]
    for half in range(2):
        mine = range(half * steps // 2, (half + 1) * steps // 2)
        given = agg_grad_ref[pl.ds(half * nets // 2, nets // 2), :]
        for at in range(0, nets, BLOCK):
            rows = pl.ds(at, BLOCK)
            parts = jnp.concatenate([own_ref[i, rows, :] for i in mine], 1)
            total = sum_ref[rows, :] + mm(parts, given)
            if half == 0:
                sum_ref[rows, :] = total
                continue
            out_ref[rows, :] = ((total + rest_ref[rows, :]) * scale).astype(bf16)
            if (at + BLOCK) * PARTS % nets == 0:
                out_ref.flush(at + BLOCK)


SM = pl.BlockSpec(memory_space=pltpu.SMEM)
VM = pl.BlockSpec(memory_space=pltpu.VMEM)
ANY = pl.BlockSpec(memory_space=pl.ANY)
SMALL = pl.CostEstimate(flops=1, bytes_accessed=1, transcendentals=0)
PARTS = 4


def shape(dims, dtype):
    return jax.ShapeDtypeStruct(dims, dtype)


def in_hbm(dims, dtype):
    return pltpu.MemorySpace.HBM(dims, dtype)


class Load:
    def __init__(self, source, target, sems, parts):
        self.target, self.shape, self.waited = target, source.shape, 0
        self.rows = source.shape[0] // parts
        self.copies = []
        for at in range(parts):
            part = pl.ds(at * self.rows, self.rows)
            self.copies.append(
                pltpu.make_async_copy(source.at[part], target.at[part], sems.at[at])
            )
            self.copies[-1].start()

    def wait(self, upto=None):
        upto = self.shape[0] if upto is None else upto
        while self.waited * self.rows < upto:
            self.copies[self.waited].wait()
            self.waited += 1

    def __getitem__(self, index):
        first = index[0] if isinstance(index, tuple) else index
        self.wait(first + 1 if isinstance(first, int) else None)
        return self.target[index]


class Store:
    def __init__(self, source, target, sems):
        self.source, self.target, self.sems = source, target, sems
        self.shape, self.dtype = source.shape, source.dtype
        self.copies, self.sent = [], 0

    def __setitem__(self, index, value):
        self.source[index] = value

    def __getitem__(self, index):
        return self.source[index]

    def flush(self, upto=None):
        upto = self.shape[0] if upto is None else upto
        part = pl.ds(self.sent, upto - self.sent)
        self.copies.append(
            pltpu.make_async_copy(
                self.source.at[part], self.target.at[part], self.sems.at[len(self.copies)]
            )
        )
        self.copies[-1].start()
        self.sent = upto

    def finish(self):
        if self.sent < self.shape[0]:
            self.flush()
        for copy in self.copies:
            copy.wait()


def call(kernel, name, outs, args, scratch=(), mib=32, flops=1, halves=-1):
    ins = [kind for _, kind in args]
    kinds = [kind for _, _, kind in outs]
    staged = [pltpu.VMEM(value.shape, value.dtype) for value, kind in args if kind == "H"]
    staged += [pltpu.VMEM(dims, dtype) for dims, dtype, kind in outs if kind == "H"]
    moved = len(staged)

    def body(*refs):
        operands, refs = list(refs[: len(ins)]), refs[len(ins) :]
        results, refs = list(refs[: len(kinds)]), refs[len(kinds) :]
        buffers, refs = list(refs[:moved]), refs[moved:]
        if moved:
            sems, refs = refs[0], refs[1:]
        at = 0
        for i, kind in enumerate(ins):
            if kind == "H":
                parts = 2 if i == halves else 1
                operands[i] = Load(operands[i], buffers[at], sems.at[at], parts)
                at += 1
        for i, kind in enumerate(kinds):
            if kind == "H":
                results[i] = Store(buffers[at], results[i], sems.at[at])
                at += 1
        kernel(*operands, *results, *refs)
        for operand in operands:
            if isinstance(operand, Load):
                operand.wait()
        for result in results:
            if isinstance(result, Store):
                result.finish()

    spec_of = {"V": VM, "H": ANY, "S": SM, "A": ANY}
    return pl.pallas_call(
        body,
        out_shape=[(in_hbm if kind == "H" else shape)(dims, dtype) for dims, dtype, kind in outs],
        in_specs=[spec_of[kind] for kind in ins],
        out_specs=[spec_of[kind] for kind in kinds],
        scratch_shapes=staged
        + ([pltpu.SemaphoreType.DMA((moved, 2 * PARTS))] if moved else [])
        + list(scratch),
        compiler_params=pltpu.CompilerParams(vmem_limit_bytes=mib << 20),
        cost_estimate=pl.CostEstimate(flops=flops, bytes_accessed=1, transcendentals=0),
        name=name,
    )(
        *[
            pltpu.with_memory_space_constraint(value, pltpu.HBM) if kind == "H" else value
            for value, kind in args
        ]
    )


def exchange(value, axis):
    return lax.all_to_all(value, axis, split_axis=0, concat_axis=0, tiled=True)


def local(
    embeds,
    neighbours,
    halo_send,
    gnn_weight,
    pair_local,
    pair_remote,
    pair_count,
    targets,
    pair_w1,
    pair_w2,
):
    nets, feat = embeds.shape
    hid = pair_w1.shape[1]
    degree = neighbours.shape[1]
    regions, slots = pair_local.shape
    peers, halo = halo_send.shape
    halo_rows = peers * halo
    devices = lax.axis_size("region") * lax.axis_size("dom")
    my_region = lax.axis_index("region").astype(i32)
    rid = my_region.reshape(1)
    cid = lax.axis_index("dom").astype(i32).reshape(1)
    near = 2
    far = regions - near
    share = 2 * feat // devices

    def permute(value, k, axis="region"):
        size = lax.axis_size(axis)
        return lax.ppermute(value, axis, [(i, i ^ k) for i in range(size)])

    def v(*values):
        return [(value, "V") for value in values]

    def h(*values):
        return [(value, "H") for value in values]

    def out(kind, dtype, *dims):
        return [(dims, dtype, kind)]

    (outgoing,) = call(
        halo_gather_kernel,
        "halo_gather",
        out("V", bf16, halo_rows, feat),
        h(halo_send, embeds),
    )
    received = exchange(outgoing.reshape(peers, halo, feat), "dom").reshape(halo_rows, feat)

    wanted = [lax.dynamic_slice_in_dim(pair_remote, my_region ^ k, 1, 0) for k in range(regions)]
    asked = [wanted[0]] + [permute(wanted[k], k) for k in range(1, regions)]

    steps = nets // STEP
    own, from_halo, agg_sum = pl.pallas_call(
        adjacency_kernel,
        grid=(steps,),
        in_specs=[
            pl.BlockSpec((degree, STEP), lambda i: (0, i)),
            pl.BlockSpec((nets, feat), lambda i: (0, 0)),
        ],
        out_specs=[
            pl.BlockSpec((1, nets, STEP), lambda i: (i, 0, 0)),
            pl.BlockSpec((1, halo_rows, STEP), lambda i: (i, 0, 0)),
            pl.BlockSpec((STEP, feat), lambda i: (i, 0)),
        ],
        out_shape=[
            in_hbm((steps, nets, STEP), bf16),
            in_hbm((steps, halo_rows, STEP), bf16),
            in_hbm((nets, feat), f32),
        ],
        scratch_shapes=[pltpu.VMEM((feat, nets), bf16)],
        compiler_params=pltpu.CompilerParams(vmem_limit_bytes=24 << 20),
        cost_estimate=SMALL,
        name="adjacency",
    )(neighbours.T, embeds)

    pre, aggregate, net_values, *far_sends = call(
        functools.partial(layer_kernel, degree=degree, far=far),
        "layer",
        out("V", f32, nets, feat)
        + out("H", bf16, nets, feat)
        + out("V", bf16, nets, feat)
        + out("V", bf16, slots, feat) * far,
        h(from_halo, agg_sum) + v(embeds, gnn_weight, received, *asked[near:]),
        [pltpu.VMEM((far, slots, nets), bf16)],
    )
    victim, linear_own, slope, *near_sends = call(
        functools.partial(victim_kernel, near=near),
        "victims",
        out("H", bf16, regions, slots, feat)
        + out("V", f32, regions, slots, hid)
        + out("H", bf16, nets, feat)
        + out("V", bf16, slots, feat) * near,
        [(rid, "S")] + v(pair_local, net_values) + h(pair_w1) + v(pre, *asked[:near]),
        flops=VICTIMS,
    )
    partners = [near_sends[0]]
    partners += [permute(near_sends[k], k) for k in range(1, near)]
    partners += [permute(far_sends[k - near], k) for k in range(near, regions)]

    groups = [tuple(range(near, regions)), tuple(range(near))]
    w2_row = pair_w2.reshape(1, hid)
    lin_grads, backs, sums = [], {}, []
    for ks in groups:
        last = ks is groups[-1]
        pieces = 2 if last else 1
        lin_grad, sums_now, *back = call(
            functools.partial(pair_kernel, ks=ks, first=ks is groups[0], last=last),
            "pairs",
            out("H", bf16, len(ks), slots, hid)
            + (out("V", bf16, devices, share + 8, hid) if last else out("V", f32, 8, hid))
            + out("V", bf16, slots // pieces, feat) * (pieces * len(ks)),
            [(rid, "S"), (pair_count, "S")]
            + v(targets, linear_own, pair_w1, w2_row)
            + v(*[partners[k] for k in ks])
            + (h(victim, *partners[near:], *lin_grads) if last else [])
            + v(*sums),
            flops=PAIRS,
        )
        lin_grads.append(lin_grad)
        for at, k in enumerate(ks):
            backs[k] = back[at * pieces : (at + 1) * pieces]
        sums = [sums_now]
    returned = [backs[0]] + [[permute(x, k) for x in backs[k]] for k in range(1, regions)]

    (w1_parts,) = sums
    w1_got = exchange(w1_parts, BOTH)
    (local_grad,) = call(
        functools.partial(local_grad_kernel, groups=groups, near=near),
        "local_grads",
        out("H", bf16, nets, feat),
        [(rid, "S")]
        + v(pair_local)
        + h(pair_w1)
        + [(w1_parts, "A")]
        + v(*asked[:near], *sum(returned[:near], []))
        + h(*lin_grads),
        [pltpu.VMEM((regions * slots, feat), bf16), pltpu.VMEM((nets, feat), f32)],
        flops=LOCAL,
    )
    order = [0, 1, *range(peers - 1, 1, -1)]
    rest, agg_grad, gnn_part, *backs = call(
        functools.partial(layer_grad_kernel, far=far, order=order, degree=degree),
        "layer_grad",
        out("H", bf16, nets, feat) * 2
        + out("H", bf16, 2 * feat, feat)
        + out("V", bf16, halo, feat) * peers,
        [(cid, "S")]
        + h(local_grad, slope)
        + v(gnn_weight, embeds)
        + h(aggregate, from_halo)
        + v(*asked[near:], *sum(returned[near:], [])),
        [pltpu.VMEM((halo_rows, feat), bf16), pltpu.VMEM((nets, feat), f32)],
        flops=10**10,
    )
    gnn_part, w1_got = lax.optimization_barrier((gnn_part, w1_got))
    gnn_got = exchange(gnn_part.reshape(devices, share, feat), BOTH)
    backs = dict(zip(order, backs, strict=True))
    returned_halo = [backs[0]] + [permute(backs[k], k, "dom") for k in range(1, peers)]

    wide, short = call(
        functools.partial(share_kernel, nets_total=nets * devices, doms=peers),
        "shares",
        out("V", bf16, devices, share, feat) + out("V", f32, 8, hid),
        v(w1_got, gnn_got),
        flops=SHARES,
    )
    spread = exchange(wide, BOTH)

    embeds_grad, w2_grad, loss = call(
        final_kernel,
        "embeds_grads",
        out("H", bf16, nets, feat) + out("V", f32, 1, hid) * 2,
        [(cid, "S")] + v(short, halo_send) + h(agg_grad, own, rest) + v(*returned_halo),
        [pltpu.VMEM((nets, feat), f32)],
        flops=FINAL,
        halves=4,
    )
    spread, w2_grad = lax.optimization_barrier((spread, w2_grad))
    w1_grad, gnn_grad = call(
        unpack_kernel,
        "unpack",
        out("H", f32, 2 * feat, hid) + out("H", f32, 2 * feat, feat),
        [(rid, "S")] + v(spread, permute(spread, 1)),
    )
    return embeds_grad, gnn_grad, w1_grad, w2_grad[0], loss[0, 0]


def solution(mesh):
    split = P(BOTH, None)
    in_specs = (split, split, split, P(), split, split, split, split, P(), P())
    out_specs = (split, P(), P(), P(), P())
    return jax.shard_map(local, mesh=mesh, in_specs=in_specs, out_specs=out_specs, check_vma=False)
```
